256 devices in a mesh: band: 32 (over z, x_lo, core), mem: 8 (over x_hi, y).
Axes of the slice: x: 4 (x_hi: 2, x_lo: 2; x = x_hi * 2 + x_lo), y: 4, z: 8, core: 2. Of those that a mesh axis runs over, the one named last changes fastest.
Arguments:
- hidden: bfloat16 [8, 16384, 1024], P('mem', 'band'), may hold values from -6 to 6
- gain: float32 [1024], replicated, may hold values from 0.5 to 1.5
- w_first: bfloat16 [1024, 1024], replicated, may hold values from -0.1875 to 0.1875
- w_second: bfloat16 [1024, 100], replicated, may hold values from -0.1875 to 0.1875
- target: float32 [100, 16384], P(None, 'band'), may hold values from -20 to 20
- patch_ids: int32 [16384], P('band'), may hold values from 0 to 63, as said below
- neighbours: int32 [6, 16384], P(None, 'band'), may hold values from 0 to 767, as said below
Outputs:
- loss: float32 [], replicated
- grad_hidden: bfloat16 [8, 16384, 1024], P('mem', 'band')
- grad_first: float32 [1024, 1024], P('band')
- grad_second: float32 [1024, 100], P('band')
The draws below stay inside these ranges and needn't reach their ends.
Inputs may be any that keep to these rules, and one draw needn't show every extreme that they name: `patch_ids`: patches of band b are numbered b * 2 onward; every patch holds exactly 256 cells, all of one band. Index j stands for local cell j - 128; values under 128 are the previous band's last cells, values of 640 and over are the next band's first cells. A cell's neighbours lie within 128 cells of it.
All inputs are finite; a program needn't handle non-finite values.
Results may differ from the reference program's by a relative error of at most 0.02.
Values may be sent and summed in bfloat16 or wider, within the bound.
No kernel may reach another device: no remote copies, remote signals or barrier semaphores. Data moves between devices by JAX's collectives and lax.ppermute only.
A program may use at most 64 MiB of HBM per device.

```python
import math
import jax
import jax.numpy as jnp
from jax import lax

H = 1024
F = 100
PATCH = 256
NEIGH = 6
HALO = 128
MEMBERS = 8
CELLS_DEV = 512
NCELL = 16384
NPATCH = 64


def draw_hidden(key, part):
    key = jax.random.fold_in(key, 14)
    subkeys = jax.random.split(key, 4)
    common = jax.random.normal(subkeys[0], (1, NCELL, H), jnp.float32)
    member_part = jax.random.normal(subkeys[1], (MEMBERS, NCELL, H), jnp.float32)
    outlier = jax.random.randint(subkeys[2], (), 0, MEMBERS)
    amount = jnp.exp(jax.random.uniform(subkeys[3], (MEMBERS, 1, 1), jnp.float32, math.log(0.12), math.log(0.3)))
    member_index = jnp.arange(MEMBERS, dtype=jnp.int32)[:, None, None]
    amount = jnp.where(member_index == outlier, 1.0, amount)
    kept_share = jnp.sqrt(jnp.maximum(1.0 - amount * amount, 0.0))
    values = common * kept_share + member_part * amount
    return jnp.clip(values, -6.0, 6.0).astype(jnp.bfloat16)


def draw_target(key, part):
    key = jax.random.fold_in(key, 11)
    cells = jnp.arange(NCELL, dtype=jnp.float32)
    ramp = 1.0 + 2.0 * cells / max(NCELL - 1, 1)
    base = jnp.clip(jax.random.normal(key, (F, NCELL), jnp.float32), -5.0, 5.0)
    return (base * ramp[None, :]).astype(jnp.float32)


def draw_patch_ids(key, part):
    key = jax.random.fold_in(key, 12)
    bands = NCELL // CELLS_DEV
    keys = jax.random.split(key, bands)
    perms = jax.vmap(lambda one: jax.random.permutation(one, CELLS_DEV))(keys)
    local = perms // PATCH
    offsets = jnp.arange(bands, dtype=jnp.int32)[:, None] * (CELLS_DEV // PATCH)
    return (local + offsets).reshape(NCELL).astype(jnp.int32)


def draw_neighbours(key, part):
    key = jax.random.fold_in(key, 13)
    offset = jax.random.randint(key, (NEIGH, NCELL), -HALO, HALO + 1)
    local = jnp.arange(NCELL, dtype=jnp.int32) % CELLS_DEV
    first_row = jnp.where(local == 0, -HALO, jnp.where(local == CELLS_DEV - 1, HALO, offset[0]))
    offset = offset.at[0].set(first_row)
    return (HALO + local[None, :] + offset).astype(jnp.int32)


def bell_draw(key, shape, deviation, limit, kind=jnp.bfloat16):
    values = deviation * jax.random.normal(key, shape, jnp.float32)
    return jnp.clip(values, min=-limit, max=limit).astype(kind)


def setup_inputs(seed: int = 0) -> dict:
    arg_keys = jax.random.split(jax.random.key(seed), 8)
    hidden = draw_hidden(jax.random.fold_in(arg_keys[7], 71), 0)
    gain = jnp.clip(1.0 + 0.1 * jax.random.normal(arg_keys[1], (H,), jnp.float32), 0.5, 1.5)
    w_first = bell_draw(arg_keys[2], (H, H), H ** -0.5, 0.1875)
    w_second = bell_draw(arg_keys[3], (H, F), H ** -0.5, 0.1875)
    target = draw_target(jax.random.fold_in(arg_keys[7], 71), 0)
    patch_ids = draw_patch_ids(jax.random.fold_in(arg_keys[7], 71), 0)
    neighbours = draw_neighbours(jax.random.fold_in(arg_keys[7], 71), 0)
    return dict(hidden=hidden, gain=gain, w_first=w_first, w_second=w_second, target=target, patch_ids=patch_ids, neighbours=neighbours)


EPS_NORM = 1e-05
EPS_DIST = 1e-06

def layer_stats(summed, gain):
    mean_value = lax.optimization_barrier(jnp.mean(summed, -1, keepdims=True))
    centred = summed - mean_value
    inv_root = lax.rsqrt(lax.optimization_barrier(jnp.mean(centred * centred, -1, keepdims=True)) + EPS_NORM)
    normal_part = centred * inv_root
    normed = (normal_part * gain).astype(jnp.bfloat16)
    return (normed, normal_part, inv_root)

def gelu_slope(preact):
    return 0.5 * (1.0 + lax.erf(preact / math.sqrt(2.0))) + preact * jnp.exp(-0.5 * preact * preact) / math.sqrt(2.0 * math.pi)

def score_patches(predicted, goal):
    members = predicted.shape[0]
    entries = predicted.shape[1] * predicted.shape[3]
    error = predicted - goal[None]
    spread_target = jnp.sqrt(lax.optimization_barrier(jnp.sum(error * error, axis=(1, 3))) / entries + EPS_DIST)
    gradient = error / (members * spread_target[:, None, :, None])
    pair_total = jnp.zeros(spread_target.shape, spread_target.dtype)
    member_ids = jnp.arange(members)
    for other in range(members):
        differ = predicted - predicted[other][None]
        spread_pair = jnp.sqrt(lax.optimization_barrier(jnp.sum(differ * differ, axis=(1, 3))) / entries + EPS_DIST)
        keep = (member_ids != other).astype(spread_pair.dtype)
        pair_total = pair_total + spread_pair * keep[:, None]
        gradient = gradient - differ / (members * (members - 1) * spread_pair[:, None, :, None])
    scores = lax.optimization_barrier(jnp.mean(spread_target, 0)) - lax.optimization_barrier(jnp.sum(pair_total, 0)) / (2 * members * (members - 1))
    return (gradient, scores)

def reference(hidden, gain, w_first, w_second, target, patch_ids, neighbours):
    members = hidden.shape[0]
    starts = jnp.arange(NCELL, dtype=jnp.int32) // CELLS_DEV * CELLS_DEV
    where_from = (neighbours + starts[None, :]).astype(jnp.int32)

    def forward(rows):
        padded = jnp.pad(rows, ((HALO, HALO), (0, 0)))
        total = jnp.zeros(rows.shape, jnp.float32)
        for neighbour in range(NEIGH):
            total = total + padded[where_from[neighbour]].astype(jnp.float32)
        summed = rows.astype(jnp.float32) + total / NEIGH
        normed, normal_part, inv_root = layer_stats(summed, gain)
        preact = jnp.dot(normed, w_first, preferred_element_type=jnp.float32)
        active = jax.nn.gelu(preact, approximate=False).astype(jnp.bfloat16)
        predicted = jnp.dot(active, w_second, preferred_element_type=jnp.float32).astype(jnp.bfloat16).T
        return (predicted, (normed, normal_part, inv_root, preact, active))
    predictions = lax.map(lambda rows: forward(rows)[0], hidden)
    order = jnp.argsort(patch_ids, stable=True).astype(jnp.int32)
    inverse = jnp.argsort(order).astype(jnp.int32)
    grouped = predictions[:, :, order].astype(jnp.float32).reshape(members, F, NPATCH, PATCH)
    goal = target[:, order].reshape(F, NPATCH, PATCH)
    gradient, scores = score_patches(grouped, goal)
    loss = jnp.sum(scores) / NPATCH
    cotangent = gradient.reshape(members, F, NCELL)[:, :, inverse]

    def backward(carry, inputs):
        rows, outer = inputs
        unused, saved = forward(rows)
        normed, normal_part, inv_root, preact, active = saved
        outer_low = outer.astype(jnp.bfloat16)
        second = jnp.dot(active.T, outer_low.T, preferred_element_type=jnp.float32)
        d_active = jnp.dot(outer_low.T, w_second.T, preferred_element_type=jnp.float32)
        d_pre = (d_active * gelu_slope(preact)).astype(jnp.bfloat16)
        first = jnp.dot(normed.T, d_pre, preferred_element_type=jnp.float32)
        d_normed = jnp.dot(d_pre, w_first.T, preferred_element_type=jnp.float32)
        scaled_grad = d_normed * gain
        d_summed = inv_root * (scaled_grad - lax.optimization_barrier(jnp.mean(scaled_grad, -1, keepdims=True)) - normal_part * lax.optimization_barrier(jnp.mean(scaled_grad * normal_part, -1, keepdims=True)))
        spread = d_summed / NEIGH
        back = jnp.zeros((NCELL + 2 * HALO, H), jnp.float32)
        for neighbour in range(NEIGH):
            back = back.at[where_from[neighbour]].add(spread)
        d_rows = (d_summed + back[HALO:HALO + NCELL]).astype(jnp.bfloat16)
        return ((carry[0] + first, carry[1] + second), d_rows)
    start_carry = (jnp.zeros((H, H), jnp.float32), jnp.zeros((H, F), jnp.float32))
    sums, grad_hidden = lax.scan(backward, start_carry, (hidden, cotangent))
    return (loss, grad_hidden, sums[0], sums[1])
```

```python
import functools
import math

import jax
import jax.numpy as jnp
from jax import lax
from jax.experimental import pallas as pl
from jax.experimental.pallas import tpu as pltpu
from jax.sharding import PartitionSpec as P

PATCH = 256
NEIGH = 6
HALO = 128
EPS_NORM = 1e-05
EPS_DIST = 1e-06
LANES = 128
F32 = jnp.float32
BF16 = jnp.bfloat16
VMEM = pl.BlockSpec(memory_space=pltpu.VMEM)


def dot(a, b, ca=1, cb=0):
    return lax.dot_general(a, b, (((ca,), (cb,)), ((), ())), preferred_element_type=F32)


def call(kernel, outs, args, flops, scratch=(), aliases=None):
    moved = sum(math.prod(a.shape) * a.dtype.itemsize for a in list(args) + list(outs))
    return pl.pallas_call(
        kernel,
        out_shape=outs,
        in_specs=[VMEM] * len(args),
        out_specs=[VMEM] * len(outs),
        scratch_shapes=list(scratch),
        input_output_aliases=aliases or {},
        compiler_params=pltpu.CompilerParams(vmem_limit_bytes=48 * 2**20),
        cost_estimate=pl.CostEstimate(flops=flops, bytes_accessed=moved, transcendentals=0),
    )(*args)


def shape(dims, kind):
    return jax.ShapeDtypeStruct(dims, kind)


def count_kernel(near_ref, counts_ref, turned_ref):
    near = near_ref[...]
    cells = near.shape[1]
    rows = cells + 2 * HALO
    for start in range(0, rows, HALO):
        place = lax.broadcasted_iota(jnp.int32, (HALO, cells), 0) + start
        total = jnp.zeros((HALO, cells), F32)
        for k in range(NEIGH):
            total = total + jnp.where(near[k : k + 1, :] == place, 1.0, 0.0)
        turned_ref[start : start + HALO, :] = total.astype(BF16)
        counts_ref[:, start : start + HALO] = total.T.astype(BF16)


def forward_kernel(
    before_ref, states_ref, after_ref, counts_ref, gain_ref, first_ref, second_ref,
    copies_ref, slope_ref, active_ref, normed_ref, inv_ref,
):
    cells, width = states_ref.shape
    rows = 128
    gain = gain_ref[...]
    for r in range(0, cells, rows):
        own = slice(r, r + rows)
        total = dot(counts_ref[own, HALO : HALO + cells], states_ref[...])
        total = total + dot(counts_ref[own, :HALO], before_ref[...])
        total = total + dot(counts_ref[own, HALO + cells :], after_ref[...])
        summed = states_ref[own, :].astype(F32) + total * (1.0 / NEIGH)
        centred = summed - jnp.mean(summed, -1, keepdims=True)
        inv_root = lax.rsqrt(jnp.mean(centred * centred, -1, keepdims=True) + EPS_NORM)
        normed_ref[own, :] = (centred * inv_root * gain).astype(BF16)
        inv_ref[own, :] = jnp.broadcast_to(inv_root, (rows, LANES))
    cols = 256
    for n in range(0, width, cols):
        part = slice(n, n + cols)
        preact = dot(normed_ref[...], first_ref[:, part])
        share = 0.5 * (1.0 + lax.erf(preact * math.sqrt(0.5)))
        active_ref[:, part] = (preact * share).astype(BF16)
        bell = jnp.exp(-0.5 * preact * preact) * (1.0 / math.sqrt(2.0 * math.pi))
        slope_ref[:, part] = (share + preact * bell).astype(BF16)
    predicted = dot(second_ref[...], active_ref[...], 0, 1).astype(BF16)
    for m in range(copies_ref.shape[0]):
        copies_ref[m] = predicted


def split_loss(tile, loss, fields):
    lane = lax.broadcasted_iota(jnp.int32, tile.shape, 1)
    high = loss.astype(BF16).astype(F32)
    low = loss - high
    return jnp.where(lane == fields, high, jnp.where(lane == fields + 1, low, tile))


def read_loss(tile, fields):
    lane = lax.broadcasted_iota(jnp.int32, tile.shape, 1)
    here = (lane == fields) | (lane == fields + 1)
    return jnp.sum(jnp.where(here, tile, 0.0), axis=1, keepdims=True)


def score_kernel(
    everyone_ref, target_ref, patch_ref, second_ref, slope_ref, active_ref, normed_ref,
    keep_ref, send_ref, dpre_ref, held_ref,
):
    members, fields, cells = everyone_ref.shape
    width = slope_ref.shape[1]
    me = lax.axis_index("mem")
    core = lax.axis_index("band") % 2
    entries = fields * PATCH
    own = everyone_ref[me].astype(F32)
    error = own - target_ref[...]
    sums = [jnp.sum(error * error, axis=0, keepdims=True)]
    for n in range(members):
        differ = own - everyone_ref[n].astype(F32)
        sums.append(jnp.sum(differ * differ, axis=0, keepdims=True))
    sums.append(jnp.zeros((16 - len(sums), cells), F32))
    sums = jnp.concatenate(sums, 0)
    even = (patch_ref[...] & 1) == 0
    spread_even = jnp.sqrt(jnp.sum(jnp.where(even, sums, 0.0), 1, keepdims=True) / entries + EPS_DIST)
    spread_odd = jnp.sqrt(jnp.sum(jnp.where(even, 0.0, sums), 1, keepdims=True) / entries + EPS_DIST)
    row = lax.broadcasted_iota(jnp.int32, (16, 1), 0)
    weight = jnp.where(row == 0, 1.0 / members, 1.0 / (members * (members - 1)))
    scale = jnp.where(even, weight / spread_even, weight / spread_odd)
    gradient = error * scale[0:1]
    for n in range(members):
        differ = own - everyone_ref[n].astype(F32)
        gradient = gradient - differ * scale[n + 1 : n + 2]
    both = spread_even + spread_odd
    used = jnp.where(row == 0, 1.0 / members, -0.5 / (members * (members - 1)))
    used = jnp.where((row == me + 1) | (row > members), 0.0, used)
    loss = jnp.sum(both * used, axis=0, keepdims=True)

    gradient = jnp.concatenate([gradient, jnp.zeros((LANES - fields, cells), F32)], 0)
    outer = gradient.T.astype(BF16)
    cols = 256
    for n in range(0, width, cols):
        part = slice(n, n + cols)
        d_active = dot(outer[:, :fields], second_ref[part, :], 1, 1)
        d_pre = (d_active * slope_ref[:, part].astype(F32)).astype(BF16)
        dpre_ref[:, part] = d_pre
        grad = dot(normed_ref[...], d_pre, 0, 0).astype(BF16)
        held_ref[:, :, part] = grad.reshape(held_ref.shape[0], -1, cols)
    second = dot(active_ref[...], outer, 0, 0)
    second = split_loss(second, loss, fields).astype(BF16)
    held_ref[:, :, width:] = second.reshape(held_ref.shape[0], -1, LANES)
    for k in range(keep_ref.shape[0]):
        keep_ref[k] = held_ref[2 * k + core]
        send_ref[k] = held_ref[2 * k + 1 - core]


def backward_kernel(
    dpre_ref, first_ref, normed_ref, gain_ref, inv_ref, turned_ref,
    grad_ref, edge_ref, up_ref, down_ref, total_ref, low_ref,
):
    cells, width = dpre_ref.shape
    rows = 128
    gain = gain_ref[...]
    for r in range(0, cells, rows):
        own = slice(r, r + rows)
        d_normed = dot(dpre_ref[own, :], first_ref[...], 1, 1)
        scaled = d_normed * gain
        normed = normed_ref[own, :].astype(F32)
        mean = jnp.mean(scaled, -1, keepdims=True)
        along = jnp.mean(d_normed * normed, -1, keepdims=True)
        inv_root = inv_ref[own, :1]
        d_summed = inv_root * (scaled - mean - normed / gain * along)
        total_ref[own, :] = d_summed
        low_ref[own, :] = d_summed.astype(BF16)
    up_ref[...] = (dot(turned_ref[:HALO, :], low_ref[...]) * (1.0 / NEIGH)).astype(BF16)
    down_ref[...] = (dot(turned_ref[cells + HALO :, :], low_ref[...]) * (1.0 / NEIGH)).astype(BF16)
    for r in range(0, cells, rows):
        own = slice(r, r + rows)
        back = dot(turned_ref[r + HALO : r + HALO + rows, :], low_ref[...]) * (1.0 / NEIGH)
        value = total_ref[own, :] + back
        grad_ref[own, :] = value.astype(BF16)
        if r == 0:
            edge_ref[0] = value
        if r + rows == cells:
            edge_ref[1] = value


def pair_kernel(fields, keep_ref, got_ref, out_ref):
    width = keep_ref.shape[2] - LANES
    for k in range(keep_ref.shape[0]):
        total = keep_ref[k].astype(F32) + got_ref[k].astype(F32)
        out_ref[k, :, :width] = total[:, :width].astype(BF16)
        tile = total[:, width:]
        out_ref[k, :, width:] = split_loss(tile, read_loss(tile, fields), fields).astype(BF16)


def fold_kernel(fields, parts_ref, out_ref):
    width = parts_ref.shape[2] - LANES
    total = parts_ref[0].astype(F32)
    for k in range(1, parts_ref.shape[0]):
        total = total + parts_ref[k].astype(F32)
    tile = total[:, width:]
    tile = split_loss(tile, read_loss(tile, fields), fields)
    total = jnp.concatenate([total[:, :width], tile], 1).astype(BF16)
    for m in range(out_ref.shape[0]):
        out_ref[m] = total


def last_kernel(fields, patches, parts_ref, first_ref, second_ref, loss_ref):
    width = first_ref.shape[1]
    total = parts_ref[0].astype(F32)
    for k in range(1, parts_ref.shape[0]):
        total = total + parts_ref[k].astype(F32)
    first_ref[...] = total[:, :width]
    tile = total[:, width:]
    second_ref[...] = tile[:, :fields]
    loss_ref[...] = read_loss(tile, fields)[:1, :] * (1.0 / patches)


def edge_kernel(grad_in_ref, edge_ref, before_ref, after_ref, grad_ref):
    del grad_in_ref
    step = pl.program_id(0)

    @pl.when(step == 0)
    def _():
        grad_ref[...] = (edge_ref[0] + before_ref[...].astype(F32)).astype(BF16)

    @pl.when(step == 1)
    def _():
        grad_ref[...] = (edge_ref[0] + after_ref[...].astype(F32)).astype(BF16)


def per_device(hidden, gain, w_first, w_second, target, patch_ids, neighbours):
    states = hidden[0]
    cells, width = states.shape
    fields = w_second.shape[1]
    bands, members = lax.axis_size("band"), lax.axis_size("mem")
    peers = bands // 2
    share = width // bands
    up = [(i, i + 1) for i in range(bands - 1)]
    down = [(j, i) for i, j in up]
    before = lax.ppermute(states[cells - HALO :], "band", up)
    after = lax.ppermute(states[:HALO], "band", down)
    gain = gain[None]
    counts, turned = call(
        count_kernel,
        [shape((cells, cells + 2 * HALO), BF16), shape((cells + 2 * HALO, cells), BF16)],
        [neighbours],
        10**8,
    )
    copies, slope, active, normed, inv_root = call(
        forward_kernel,
        [
            shape((members, fields, cells), BF16),
            shape((cells, width), BF16),
            shape((cells, width), BF16),
            shape((cells, width), BF16),
            shape((cells, LANES), F32),
        ],
        [before, states, after, counts, gain, w_first, w_second],
        2 * 10**9,
    )
    everyone = lax.all_to_all(copies, "mem", 0, 0)
    message = (peers, share, width + LANES)
    keep, send, d_pre = call(
        score_kernel,
        [shape(message, BF16), shape(message, BF16), shape((cells, width), BF16)],
        [everyone, target, patch_ids[None], w_second, slope, active, normed],
        2 * 10**9,
        scratch=[pltpu.VMEM((bands, share, width + LANES), BF16)],
    )
    got = lax.ppermute(send, "band", [(i, i ^ 1) for i in range(bands)])
    grad, edge, rim_up, rim_down = call(
        backward_kernel,
        [
            shape((cells, width), BF16),
            shape((2, HALO, width), F32),
            shape((HALO, width), BF16),
            shape((HALO, width), BF16),
        ],
        [d_pre, w_first, normed, gain, inv_root, turned],
        2 * 10**9,
        scratch=[pltpu.VMEM((cells, width), F32), pltpu.VMEM((cells, width), BF16)],
    )
    rim_after = lax.ppermute(rim_up, "band", down)
    rim_before = lax.ppermute(rim_down, "band", up)
    (mine,) = call(
        functools.partial(pair_kernel, fields), [shape(message, BF16)], [keep, got], 10**6
    )
    groups = [[2 * k + c for k in range(peers)] for c in range(2)]
    parts = lax.all_to_all(mine, "band", 0, 0, axis_index_groups=groups)
    (shared,) = call(
        functools.partial(fold_kernel, fields),
        [shape((members,) + message[1:], BF16)],
        [parts],
        10**6,
    )
    parts = lax.all_to_all(shared, "mem", 0, 0)
    grad_first, grad_second, loss = call(
        functools.partial(last_kernel, fields, cells // PATCH * bands),
        [shape((share, width), F32), shape((share, fields), F32), shape((1, 1), F32)],
        [parts],
        10**6,
    )
    last = cells // HALO - 1
    grad_hidden = pl.pallas_call(
        edge_kernel,
        grid=(2,),
        out_shape=shape((cells, width), BF16),
        in_specs=[
            pl.BlockSpec(memory_space=pl.ANY),
            pl.BlockSpec((1, HALO, width), lambda i: (i, 0, 0)),
            pl.BlockSpec((HALO, width), lambda i: (0, 0)),
            pl.BlockSpec((HALO, width), lambda i: (0, 0)),
        ],
        out_specs=pl.BlockSpec((HALO, width), lambda i: (i * last, 0)),
        input_output_aliases={0: 0},
        compiler_params=pltpu.CompilerParams(vmem_limit_bytes=16 * 2**20),
    )(grad, edge, rim_before, rim_after)
    return (loss[0, 0], grad_hidden[None], grad_first, grad_second)


def solution(mesh):
    return jax.shard_map(
        per_device,
        mesh=mesh,
        in_specs=(
            P("mem", "band", None),
            P(),
            P(),
            P(),
            P(None, "band"),
            P("band"),
            P(None, "band"),
        ),
        out_specs=(P(), P("mem", "band", None), P("band", None), P("band", None)),
        check_vma=False,
    )
```

```python
import functools
import math

import jax
import jax.numpy as jnp
from jax import lax
from jax.experimental import pallas as pl
from jax.experimental.pallas import tpu as pltpu
from jax.sharding import PartitionSpec as P

PATCH = 256
NEIGH = 6
HALO = 128
EPS_NORM = 1e-05
EPS_DIST = 1e-06
LANES = 128
F32 = jnp.float32
BF16 = jnp.bfloat16
VMEM = pl.BlockSpec(memory_space=pltpu.VMEM)
ANY = pl.BlockSpec(memory_space=pl.ANY)


def dot(a, b, ca=1, cb=0):
    return lax.dot_general(a, b, (((ca,), (cb,)), ((), ())), preferred_element_type=F32)


def call(kernel, outs, args, flops, limit, scratch=(), anywhere=(), stored=(), held=()):
    args = [
        pltpu.with_memory_space_constraint(a, pltpu.HBM) if i in anywhere else a
        for i, a in enumerate(args)
    ]
    moved = sum(math.prod(a.shape) * a.dtype.itemsize for a in list(args) + list(outs))
    return pl.pallas_call(
        kernel,
        out_shape=[
            pltpu.HBM(o.shape, o.dtype) if i in stored else pltpu.VMEM(o.shape, o.dtype) if i in held else o
            for i, o in enumerate(outs)
        ],
        in_specs=[ANY if i in anywhere else VMEM for i in range(len(args))],
        out_specs=[ANY if i in stored else VMEM for i in range(len(outs))],
        scratch_shapes=list(scratch),
        compiler_params=pltpu.CompilerParams(vmem_limit_bytes=limit * 2**20),
        cost_estimate=pl.CostEstimate(flops=flops, bytes_accessed=moved, transcendentals=0),
    )(*args)


def shape(dims, kind):
    return jax.ShapeDtypeStruct(dims, kind)


def count_rows(near, block):
    near = near[:, block * HALO : (block + 1) * HALO]
    place = lax.broadcasted_iota(jnp.int32, (3 * HALO, HALO), 0) + block * HALO
    total = jnp.zeros((3 * HALO, HALO), F32)
    for k in range(NEIGH):
        total = total + jnp.where(near[k : k + 1, :] == place, 1.0, 0.0)
    return total


def normalise(summed, gain):
    centred = summed - jnp.mean(summed, -1, keepdims=True)
    inv_root = lax.rsqrt(jnp.mean(centred * centred, -1, keepdims=True) + EPS_NORM)
    normed = (centred * inv_root * gain).astype(BF16)
    return normed, jnp.broadcast_to(inv_root, (summed.shape[0], LANES))


def head(normed_ref, first_ref, part):
    preact = dot(normed_ref[...], first_ref[:, part])
    share = 0.5 * (1.0 + lax.erf(preact * math.sqrt(0.5)))
    bell = jnp.exp(-0.5 * preact * preact) * (1.0 / math.sqrt(2.0 * math.pi))
    return (preact * share).astype(BF16), (share + preact * bell).astype(BF16)


def inner_kernel(
    near_ref, states_ref, gain_ref, second_ref, first_hbm,
    predicted_ref, slope_ref, active_ref, normed_ref, inv_ref, first_ref,
    done,
):
    load = pltpu.make_async_copy(first_hbm, first_ref, done)
    load.start()
    near = near_ref[...]
    for block in (1, 2):
        reach = states_ref[(block - 1) * HALO : (block + 2) * HALO, :]
        counts = count_rows(near, block).T.astype(BF16)
        own = states_ref[block * HALO : (block + 1) * HALO, :].astype(F32)
        summed = own + dot(counts, reach) * (1.0 / NEIGH)
        to = slice((block - 1) * HALO, block * HALO)
        normed_ref[to, :], inv_ref[to, :] = normalise(summed, gain_ref[...])
    load.wait()
    cols = 256
    for n in range(0, normed_ref.shape[1], cols):
        part = slice(n, n + cols)
        active_ref[:, part], slope_ref[:, part] = head(normed_ref, first_ref, part)
    predicted_ref[...] = dot(second_ref[...], active_ref[...], 1, 1).astype(BF16)


def prepare_kernel(near_ref, states_ref, partial_ref, outside_ref, turned_ref):
    near = near_ref[...]
    blocks = states_ref.shape[0] // HALO
    for block in range(blocks):
        cells = slice(block * HALO, (block + 1) * HALO)
        total = count_rows(near, block)
        turned_ref[block * HALO : (block + 3) * HALO, cells] = total.astype(BF16)
        if block in (0, blocks - 1):
            edge = 0 if block == 0 else 1
            to = slice(edge * HALO, (edge + 1) * HALO)
            counts = total.T.astype(BF16)
            inside = slice(HALO, 3 * HALO) if edge == 0 else slice(0, 2 * HALO)
            outside = slice(0, HALO) if edge == 0 else slice(2 * HALO, 3 * HALO)
            start = 0 if edge == 0 else (blocks - 2) * HALO
            reach = states_ref[start : start + 2 * HALO, :]
            partial_ref[to, :] = states_ref[cells, :].astype(F32) + dot(counts[:, inside], reach) * (
                1.0 / NEIGH
            )
            outside_ref[edge] = counts[:, outside]


def outer_kernel(
    before_ref, after_ref, partial_ref, outside_ref, gain_ref, second_ref,
    predicted_in_ref, slope_in_ref, active_in_ref, normed_in_ref, inv_in_ref, first_ref,
    copies_ref, slope_ref, active_ref, normed_ref, inv_ref,
    own_ref,
):
    cells, width = normed_ref.shape
    top, inner, bottom = slice(0, HALO), slice(HALO, cells - HALO), slice(cells - HALO, cells)
    for edge, (rows_ref, place) in enumerate(((before_ref, top), (after_ref, bottom))):
        to = slice(edge * HALO, (edge + 1) * HALO)
        summed = partial_ref[to, :] + dot(outside_ref[edge], rows_ref[...]) * (1.0 / NEIGH)
        normed, inv_ref[place, :] = normalise(summed, gain_ref[...])
        normed_ref[place, :] = normed
        own_ref[to, :] = normed
    normed_ref[inner, :] = normed_in_ref[...]
    inv_ref[inner, :] = inv_in_ref[...]
    active_ref[inner, :] = active_in_ref[...]
    slope_ref[inner, :] = slope_in_ref[...]
    cols = 256
    for n in range(0, width, cols):
        part = slice(n, n + cols)
        active, slope = head(own_ref, first_ref, part)
        active_ref[top, part] = active[:HALO]
        active_ref[bottom, part] = active[HALO:]
        slope_ref[top, part] = slope[:HALO]
        slope_ref[bottom, part] = slope[HALO:]
    own = jnp.concatenate([active_ref[top, :], active_ref[bottom, :]], 0)
    predicted = dot(second_ref[...], own, 1, 1).astype(BF16)
    for m in range(copies_ref.shape[0]):
        copies_ref[m, :, top] = predicted[:, :HALO]
        copies_ref[m, :, inner] = predicted_in_ref[...]
        copies_ref[m, :, bottom] = predicted[:, HALO:]


def split_loss(tile, loss, fields):
    lane = lax.broadcasted_iota(jnp.int32, tile.shape, 1)
    high = loss.astype(BF16).astype(F32)
    low = loss - high
    return jnp.where(lane == fields, high, jnp.where(lane == fields + 1, low, tile))


def read_loss(tile, fields):
    lane = lax.broadcasted_iota(jnp.int32, tile.shape, 1)
    here = (lane == fields) | (lane == fields + 1)
    return jnp.sum(jnp.where(here, tile, 0.0), axis=1, keepdims=True)


def score_kernel(
    everyone_ref, target_ref, patch_ref, second_ref, slope_ref, active_ref, normed_ref,
    keep_ref, send_ref, dpre_ref, held_ref,
):
    members, fields, cells = everyone_ref.shape
    width = slope_ref.shape[1]
    me = lax.axis_index("xh") * lax.axis_size("y") + lax.axis_index("y")
    core = lax.axis_index("co")
    entries = fields * PATCH
    share = held_ref.shape[3]

    def target_of(xl, member):
        return (member % 4) * 4 + (member // 4) * 2 + xl

    places = [(b, ((b // 2) % 2, b // 4)) for b in range(width // share)]
    own = everyone_ref[me].astype(F32)
    error = own - target_ref[...]
    sums = [jnp.sum(error * error, axis=0, keepdims=True)]
    for n in range(members):
        differ = own - everyone_ref[n].astype(F32)
        sums.append(jnp.sum(differ * differ, axis=0, keepdims=True))
    sums.append(jnp.zeros((16 - len(sums), cells), F32))
    sums = jnp.concatenate(sums, 0)
    even = (patch_ref[...] & 1) == 0
    spread_even = jnp.sqrt(jnp.sum(jnp.where(even, sums, 0.0), 1, keepdims=True) / entries + EPS_DIST)
    spread_odd = jnp.sqrt(jnp.sum(jnp.where(even, 0.0, sums), 1, keepdims=True) / entries + EPS_DIST)
    row = lax.broadcasted_iota(jnp.int32, (16, 1), 0)
    weight = jnp.where(row == 0, 1.0 / members, 1.0 / (members * (members - 1)))
    scale = jnp.where(even, weight / spread_even, weight / spread_odd)
    gradient = error * scale[0:1]
    for n in range(members):
        differ = own - everyone_ref[n].astype(F32)
        gradient = gradient - differ * scale[n + 1 : n + 2]
    both = spread_even + spread_odd
    used = jnp.where(row == 0, 1.0 / members, -0.5 / (members * (members - 1)))
    used = jnp.where((row == me + 1) | (row > members), 0.0, used)
    loss = jnp.sum(both * used, axis=0, keepdims=True)

    gradient = jnp.concatenate([gradient, jnp.zeros((LANES - fields, cells), F32)], 0)
    outer = gradient.T.astype(BF16)
    cols = 256
    for n in range(0, width, cols):
        part = slice(n, n + cols)
        d_active = dot(outer[:, :fields], second_ref[:, part])
        d_pre = (d_active * slope_ref[:, part].astype(F32)).astype(BF16)
        dpre_ref[:, part] = d_pre
        grad = dot(normed_ref[...], d_pre, 0, 0).astype(BF16)
        for band, slot in places:
            rows = grad[band * share : (band + 1) * share]
            for c in range(0, cols, LANES):
                block = (n + c) // LANES
                held_ref[band % 2, target_of(slot[0], block), slot[1]] = rows[:, c : c + LANES]
    second = dot(active_ref[...], outer, 0, 0)
    second = split_loss(second, loss, fields).astype(BF16)
    for band, slot in places:
        rows = second[band * share : (band + 1) * share]
        held_ref[band % 2, target_of(slot[0], slot[1]), members] = rows
    keep_ref[...] = held_ref[core]
    send_ref[...] = held_ref[1 - core]


def backward_kernel(
    first_ref, dpre_ref, normed_ref, inv_ref, turned_ref, gain_ref,
    grad_hbm, edge_hbm, up_hbm, down_hbm,
    total_ref, low_ref, grad_ref, edge_ref, rim_ref, done,
):
    cells, width = low_ref.shape
    blocks = cells // HALO
    gain = gain_ref[...]
    inverse = 1.0 / gain
    saves = [
        pltpu.make_async_copy(source, place, done.at[i])
        for i, (source, place) in enumerate(
            [
                (rim_ref.at[0], up_hbm),
                (rim_ref.at[1], down_hbm),
                (edge_ref, edge_hbm),
                (grad_ref, grad_hbm),
            ]
        )
    ]
    for block in range(blocks):
        own = slice(block * HALO, (block + 1) * HALO)
        d_normed = dot(dpre_ref[own, :], first_ref[...], 1, 1)
        scaled = d_normed * gain
        normed = normed_ref[own, :].astype(F32)
        mean = jnp.mean(scaled, -1, keepdims=True)
        along = jnp.mean(d_normed * normed, -1, keepdims=True)
        d_summed = inv_ref[own, :1] * (scaled - mean - normed * inverse * along)
        total_ref[own, :] = d_summed
        low_ref[own, :] = d_summed.astype(BF16)
    for row in (0, blocks + 1, 1, blocks, *range(2, blocks)):
        near = slice(max(row - 2, 0) * HALO, min(row + 1, blocks) * HALO)
        back = dot(turned_ref[row * HALO : (row + 1) * HALO, near], low_ref[near, :]) * (1.0 / NEIGH)
        if row in (0, blocks + 1):
            rim = 0 if row == 0 else 1
            rim_ref[rim] = back.astype(BF16)
            saves[rim].start()
            continue
        own = slice((row - 1) * HALO, row * HALO)
        value = total_ref[own, :] + back
        grad_ref[own, :] = value.astype(BF16)
        if row in (1, blocks):
            edge_ref[0 if row == 1 else 1] = value
        if row == blocks:
            saves[2].start()
    saves[3].start()
    for save in saves:
        save.wait()


def pair_kernel(fields, keep_ref, got_ref, out_ref):
    last = keep_ref.shape[1] - 1
    for k in range(keep_ref.shape[0]):
        total = keep_ref[k, :last].astype(F32) + got_ref[k, :last].astype(F32)
        out_ref[k, :last] = total.astype(BF16)
        tile = keep_ref[k, last].astype(F32) + got_ref[k, last].astype(F32)
        out_ref[k, last] = split_loss(tile, read_loss(tile, fields), fields).astype(BF16)


def plane_kernel(fields, parts_ref, out_ref):
    me = lax.axis_index("xh") * lax.axis_size("y") + lax.axis_index("y")
    blocks = parts_ref.shape[1] - 1
    for j in range(blocks + 1):
        total = parts_ref[0, j].astype(F32)
        for k in range(1, parts_ref.shape[0]):
            total = total + parts_ref[k, j].astype(F32)
        if j < blocks:
            out_ref[j, 0] = total.astype(BF16)
    loss = read_loss(total, fields)
    for j in range(blocks):
        tile = jnp.where(me == j, total, 0.0)
        out_ref[j, 1] = split_loss(tile, loss, fields).astype(BF16)


def fold_kernel(fields, parts_ref, out_ref):
    total = parts_ref[0].astype(F32)
    for k in range(1, parts_ref.shape[0]):
        total = total + parts_ref[k].astype(F32)
    first = total[0].astype(BF16)
    second = split_loss(total[1], read_loss(total[1], fields), fields).astype(BF16)
    for m in range(out_ref.shape[0]):
        out_ref[m, 0] = first
        out_ref[m, 1] = second


def last_kernel(fields, patches, parts_ref, first_ref, second_ref, loss_ref):
    for k in range(parts_ref.shape[0]):
        first_ref[:, k * LANES : (k + 1) * LANES] = parts_ref[k, 0].astype(F32)
    tile = parts_ref[lax.axis_index("z"), 1].astype(F32)
    second_ref[...] = tile[:, :fields]
    loss_ref[...] = read_loss(tile, fields)[:1, :] * (1.0 / patches)


def edge_kernel(grad_in_ref, edge_ref, before_ref, after_ref, grad_ref):
    del grad_in_ref
    step = pl.program_id(0)

    @pl.when(step == 0)
    def _():
        grad_ref[...] = (edge_ref[0] + before_ref[...].astype(F32)).astype(BF16)

    @pl.when(step == 1)
    def _():
        grad_ref[...] = (edge_ref[0] + after_ref[...].astype(F32)).astype(BF16)


BAND = ("z", "xl", "co")
MEM = ("xh", "y")
PLANE = ("y", "xh", "xl")


def per_device(hidden, gain, w_first, w_second, target, patch_ids, neighbours):
    states = hidden[0]
    cells, width = states.shape
    fields = w_second.shape[1]
    bands, members = lax.axis_size(BAND), lax.axis_size(MEM)
    share = width // bands
    up = [(i, i + 1) for i in range(bands - 1)]
    down = [(j, i) for i, j in up]
    before = lax.ppermute(states[cells - HALO :], BAND, up)
    after = lax.ppermute(states[:HALO], BAND, down)
    gain = gain[None]
    second = w_second.T
    half = cells // 2
    saved = [shape((half, width), BF16)] * 3 + [shape((half, LANES), F32)]
    inside = call(
        inner_kernel,
        [shape((fields, half), BF16)] + saved + [shape(w_first.shape, BF16)],
        [neighbours, states, gain, second, w_first],
        10**9,
        16,
        [pltpu.SemaphoreType.DMA],
        anywhere=(4,),
        held=(5,),
    )
    partial, outside, turned = call(
        prepare_kernel,
        [
            shape((half, width), F32),
            shape((2, HALO, HALO), BF16),
            shape((cells + 2 * HALO, cells), BF16),
        ],
        [neighbours, states],
        10**8,
        12,
    )
    saved = [shape((cells, width), BF16)] * 3 + [shape((cells, LANES), F32)]
    copies, slope, active, normed, inv_root = call(
        outer_kernel,
        [shape((members, fields, cells), BF16)] + saved,
        [before, after, partial, outside, gain, second, *inside],
        10**9,
        20,
        [pltpu.VMEM((half, width), BF16)],
    )
    everyone = lax.all_to_all(copies, MEM, 0, 0)
    message = (2 * members, members + 1, share, LANES)
    keep, send, d_pre = call(
        score_kernel,
        [shape(message, BF16), shape(message, BF16), shape((cells, width), BF16)],
        [everyone, target, patch_ids[None], second, slope, active, normed],
        2 * 10**9,
        20,
        [pltpu.VMEM((2,) + message, BF16)],
    )
    got = lax.ppermute(send, "co", [(0, 1), (1, 0)])
    grad, edge, rim_up, rim_down = call(
        backward_kernel,
        [
            shape((cells, width), BF16),
            shape((2, HALO, width), F32),
            shape((HALO, width), BF16),
            shape((HALO, width), BF16),
        ],
        [inside[-1], d_pre, normed, inv_root, turned, gain],
        2 * 10**9,
        20,
        [
            pltpu.VMEM((cells, width), F32),
            pltpu.VMEM((cells, width), BF16),
            pltpu.VMEM((cells, width), BF16),
            pltpu.VMEM((2, HALO, width), F32),
            pltpu.VMEM((2, HALO, width), BF16),
            pltpu.SemaphoreType.DMA((4,)),
        ],
        stored=(0, 1, 2, 3),
    )
    got, grad = lax.optimization_barrier((got, grad))
    (mine,) = call(
        functools.partial(pair_kernel, fields), [shape(message, BF16)], [keep, got], 10**6, 8
    )
    parts = lax.all_to_all(mine, PLANE, 0, 0)
    parts, rim_up, rim_down, grad = lax.optimization_barrier((parts, rim_up, rim_down, grad))
    rim_after = lax.ppermute(rim_up, BAND, down)
    rim_before = lax.ppermute(rim_down, BAND, up)
    last = cells // HALO - 1
    grad_hidden = pl.pallas_call(
        edge_kernel,
        grid=(2,),
        out_shape=shape((cells, width), BF16),
        in_specs=[
            pl.BlockSpec(memory_space=pl.ANY),
            pl.BlockSpec((1, HALO, width), lambda i: (i, 0, 0)),
            pl.BlockSpec((HALO, width), lambda i: (0, 0)),
            pl.BlockSpec((HALO, width), lambda i: (0, 0)),
        ],
        out_specs=pl.BlockSpec((HALO, width), lambda i: (i * last, 0)),
        input_output_aliases={0: 0},
        compiler_params=pltpu.CompilerParams(vmem_limit_bytes=8 * 2**20),
    )(grad, edge, rim_before, rim_after)
    message = (members, 2, share, LANES)
    (planed,) = call(
        functools.partial(plane_kernel, fields), [shape(message, BF16)], [parts], 10**6, 8
    )
    parts = lax.all_to_all(planed, "z", 0, 0)
    (folded,) = call(
        functools.partial(fold_kernel, fields), [shape(message, BF16)], [parts], 10**6, 8
    )
    parts = lax.all_to_all(folded, MEM, 0, 0)
    grad_first, grad_second, loss = call(
        functools.partial(last_kernel, fields, cells // PATCH * bands),
        [shape((share, width), F32), shape((share, fields), F32), shape((1, 1), F32)],
        [parts],
        10**6,
        8,
    )
    return (loss[0, 0], grad_hidden[None], grad_first, grad_second)


def solution(mesh):
    split = jax.sharding.Mesh(mesh.devices.reshape(8, 2, 2, 2, 4), BAND + MEM)
    return jax.shard_map(
        per_device,
        mesh=split,
        in_specs=(
            P(MEM, BAND, None),
            P(),
            P(),
            P(),
            P(None, BAND),
            P(BAND),
            P(None, BAND),
        ),
        out_specs=(P(), P(MEM, BAND, None), P(BAND, None), P(BAND, None)),
        check_vma=False,
    )
```

```python
import functools
import math

import jax
import jax.numpy as jnp
from jax import lax
from jax.experimental import pallas as pl
from jax.experimental.pallas import tpu as pltpu
from jax.sharding import PartitionSpec as P

PATCH = 256
NEIGH = 6
HALO = 128
EPS_NORM = 1e-05
EPS_DIST = 1e-06
LANES = 128
F32 = jnp.float32
BF16 = jnp.bfloat16
VMEM = pl.BlockSpec(memory_space=pltpu.VMEM)
ANY = pl.BlockSpec(memory_space=pl.ANY)


def dot(a, b, ca=1, cb=0):
    return lax.dot_general(a, b, (((ca,), (cb,)), ((), ())), preferred_element_type=F32)


def call(kernel, outs, args, flops, limit, scratch=(), anywhere=(), stored=(), held=()):
    args = [
        pltpu.with_memory_space_constraint(a, pltpu.HBM) if i in anywhere else a
        for i, a in enumerate(args)
    ]
    moved = sum(math.prod(a.shape) * a.dtype.itemsize for a in list(args) + list(outs))
    return pl.pallas_call(
        kernel,
        out_shape=[
            pltpu.HBM(o.shape, o.dtype) if i in stored else pltpu.VMEM(o.shape, o.dtype) if i in held else o
            for i, o in enumerate(outs)
        ],
        in_specs=[ANY if i in anywhere else VMEM for i in range(len(args))],
        out_specs=[ANY if i in stored else VMEM for i in range(len(outs))],
        scratch_shapes=list(scratch),
        compiler_params=pltpu.CompilerParams(vmem_limit_bytes=limit * 2**20),
        cost_estimate=pl.CostEstimate(flops=flops, bytes_accessed=moved, transcendentals=0),
    )(*args)


def shape(dims, kind):
    return jax.ShapeDtypeStruct(dims, kind)


def rims_kernel(states_hbm, same_ref, other_ref, done):
    rows = states_hbm.shape[0]
    core = lax.axis_index("co")
    low, high = core * (rows - HALO), (1 - core) * (rows - HALO)
    moves = [
        pltpu.make_async_copy(states_hbm.at[pl.ds(low, HALO)], other_ref, done.at[0]),
        pltpu.make_async_copy(states_hbm.at[pl.ds(high, HALO)], same_ref, done.at[1]),
    ]
    for move in moves:
        move.start()
    for move in moves:
        move.wait()


def count_rows(near, block):
    near = near[:, block * HALO : (block + 1) * HALO]
    place = lax.broadcasted_iota(jnp.int32, (3 * HALO, HALO), 0) + block * HALO
    total = jnp.zeros((3 * HALO, HALO), F32)
    for k in range(NEIGH):
        total = total + jnp.where(near[k : k + 1, :] == place, 1.0, 0.0)
    return total


def normalise(summed, gain):
    centred = summed - jnp.mean(summed, -1, keepdims=True)
    inv_root = lax.rsqrt(jnp.mean(centred * centred, -1, keepdims=True) + EPS_NORM)
    normed = (centred * inv_root * gain).astype(BF16)
    return normed, jnp.broadcast_to(inv_root, (summed.shape[0], LANES))


def head(normed_ref, first_ref, part):
    preact = dot(normed_ref[...], first_ref[:, part])
    share = 0.5 * (1.0 + lax.erf(preact * math.sqrt(0.5)))
    bell = jnp.exp(-0.5 * preact * preact) * (1.0 / math.sqrt(2.0 * math.pi))
    return (preact * share).astype(BF16), (share + preact * bell).astype(BF16)


def inner_kernel(
    near_hbm, states_hbm, gain_hbm, first_hbm, second_hbm,
    predicted_ref, slope_ref, active_ref, normed_ref, inv_ref, gain_ref, first_ref, second_ref,
    partial_ref, outside_ref, turned_ref,
    near_ref, states_ref, done,
):
    loads = [
        pltpu.make_async_copy(source, place, done.at[i])
        for i, (source, place) in enumerate(
            [
                (near_hbm, near_ref),
                (states_hbm, states_ref),
                (gain_hbm, gain_ref),
                (first_hbm, first_ref),
                (second_hbm, second_ref),
            ]
        )
    ]
    for load in loads:
        load.start()
    loads[0].wait()
    near = near_ref[...]
    blocks = states_ref.shape[0] // HALO
    counts = []
    for block in range(blocks):
        total = count_rows(near, block)
        turned_ref[block * HALO : (block + 3) * HALO, block * HALO : (block + 1) * HALO] = total.astype(BF16)
        counts.append(total.T.astype(BF16))
    outside_ref[0] = counts[0][:, :HALO]
    outside_ref[1] = counts[-1][:, 2 * HALO :]
    loads[1].wait()
    loads[2].wait()
    for block in range(1, blocks - 1):
        reach = states_ref[(block - 1) * HALO : (block + 2) * HALO, :]
        own = states_ref[block * HALO : (block + 1) * HALO, :].astype(F32)
        summed = own + dot(counts[block], reach) * (1.0 / NEIGH)
        to = slice((block - 1) * HALO, block * HALO)
        normed_ref[to, :], inv_ref[to, :] = normalise(summed, gain_ref[...])
    for edge, block, reach in ((0, 0, counts[0][:, HALO:]), (1, blocks - 1, counts[-1][:, : 2 * HALO])):
        start = 0 if edge == 0 else (blocks - 2) * HALO
        own = states_ref[block * HALO : (block + 1) * HALO, :].astype(F32)
        inside = dot(reach, states_ref[start : start + 2 * HALO, :])
        partial_ref[edge * HALO : (edge + 1) * HALO, :] = own + inside * (1.0 / NEIGH)
    loads[3].wait()
    loads[4].wait()
    cols = 256
    for n in range(0, normed_ref.shape[1], cols):
        part = slice(n, n + cols)
        active_ref[:, part], slope_ref[:, part] = head(normed_ref, first_ref, part)
    predicted_ref[...] = dot(second_ref[...], active_ref[...], 1, 1).astype(BF16)


def outer_kernel(
    same_ref, other_ref, partial_ref, outside_ref, gain_ref, second_ref,
    predicted_in_ref, slope_in_ref, active_in_ref, normed_in_ref, inv_in_ref, first_ref,
    copies_ref, slope_ref, active_ref, normed_ref, inv_ref,
    own_ref,
):
    cells, width = normed_ref.shape
    top, inner, bottom = slice(0, HALO), slice(HALO, cells - HALO), slice(cells - HALO, cells)
    core = lax.axis_index("co")
    for edge, place in enumerate((top, bottom)):
        to = slice(edge * HALO, (edge + 1) * HALO)
        rows = jnp.where(core == edge, other_ref[...], same_ref[...])
        summed = partial_ref[to, :] + dot(outside_ref[edge], rows) * (1.0 / NEIGH)
        normed, inv_ref[place, :] = normalise(summed, gain_ref[...])
        normed_ref[place, :] = normed
        own_ref[to, :] = normed
    normed_ref[inner, :] = normed_in_ref[...]
    inv_ref[inner, :] = inv_in_ref[...]
    active_ref[inner, :] = active_in_ref[...]
    slope_ref[inner, :] = slope_in_ref[...]
    cols = 256
    for n in range(0, width, cols):
        part = slice(n, n + cols)
        active, slope = head(own_ref, first_ref, part)
        active_ref[top, part] = active[:HALO]
        active_ref[bottom, part] = active[HALO:]
        slope_ref[top, part] = slope[:HALO]
        slope_ref[bottom, part] = slope[HALO:]
    own = jnp.concatenate([active_ref[top, :], active_ref[bottom, :]], 0)
    predicted = dot(second_ref[...], own, 1, 1).astype(BF16)
    for m in range(copies_ref.shape[0]):
        copies_ref[m, :, top] = predicted[:, :HALO]
        copies_ref[m, :, inner] = predicted_in_ref[...]
        copies_ref[m, :, bottom] = predicted[:, HALO:]


def split_loss(tile, loss, fields):
    lane = lax.broadcasted_iota(jnp.int32, tile.shape, 1)
    high = loss.astype(BF16).astype(F32)
    low = loss - high
    return jnp.where(lane == fields, high, jnp.where(lane == fields + 1, low, tile))


def read_loss(tile, fields):
    lane = lax.broadcasted_iota(jnp.int32, tile.shape, 1)
    here = (lane == fields) | (lane == fields + 1)
    return jnp.sum(jnp.where(here, tile, 0.0), axis=1, keepdims=True)


def score_kernel(
    everyone_ref, target_ref, patch_ref, second_ref, slope_ref, active_ref, normed_ref,
    keep_ref, send_ref, dpre_ref, held_ref,
):
    members, fields, cells = everyone_ref.shape
    width = slope_ref.shape[1]
    me = lax.axis_index("xh") * lax.axis_size("y") + lax.axis_index("y")
    core = lax.axis_index("co")
    entries = fields * PATCH
    share = held_ref.shape[3]

    def target_of(xl, member):
        return (member % 4) * 4 + (member // 4) * 2 + xl

    places = [(b, ((b // 2) % 2, b // 4)) for b in range(width // share)]
    own = everyone_ref[me].astype(F32)
    error = own - target_ref[...]
    sums = [jnp.sum(error * error, axis=0, keepdims=True)]
    for n in range(members):
        differ = own - everyone_ref[n].astype(F32)
        sums.append(jnp.sum(differ * differ, axis=0, keepdims=True))
    sums.append(jnp.zeros((16 - len(sums), cells), F32))
    sums = jnp.concatenate(sums, 0)
    even = (patch_ref[...] & 1) == 0
    spread_even = jnp.sqrt(jnp.sum(jnp.where(even, sums, 0.0), 1, keepdims=True) / entries + EPS_DIST)
    spread_odd = jnp.sqrt(jnp.sum(jnp.where(even, 0.0, sums), 1, keepdims=True) / entries + EPS_DIST)
    row = lax.broadcasted_iota(jnp.int32, (16, 1), 0)
    weight = jnp.where(row == 0, 1.0 / members, 1.0 / (members * (members - 1)))
    scale = jnp.where(even, weight / spread_even, weight / spread_odd)
    gradient = error * scale[0:1]
    for n in range(members):
        differ = own - everyone_ref[n].astype(F32)
        gradient = gradient - differ * scale[n + 1 : n + 2]
    both = spread_even + spread_odd
    used = jnp.where(row == 0, 1.0 / members, -0.5 / (members * (members - 1)))
    used = jnp.where((row == me + 1) | (row > members), 0.0, used)
    loss = jnp.sum(both * used, axis=0, keepdims=True)

    gradient = jnp.concatenate([gradient, jnp.zeros((LANES - fields, cells), F32)], 0)
    outer = gradient.T.astype(BF16)
    cols = 256
    for n in range(0, width, cols):
        part = slice(n, n + cols)
        d_active = dot(outer[:, :fields], second_ref[:, part])
        d_pre = (d_active * slope_ref[:, part].astype(F32)).astype(BF16)
        dpre_ref[:, part] = d_pre
        grad = dot(normed_ref[...], d_pre, 0, 0).astype(BF16)
        for band, slot in places:
            rows = grad[band * share : (band + 1) * share]
            for c in range(0, cols, LANES):
                block = (n + c) // LANES
                held_ref[band % 2, target_of(slot[0], block), slot[1]] = rows[:, c : c + LANES]
    second = dot(active_ref[...], outer, 0, 0)
    second = split_loss(second, loss, fields).astype(BF16)
    for band, slot in places:
        rows = second[band * share : (band + 1) * share]
        held_ref[band % 2, target_of(slot[0], slot[1]), members] = rows
    keep_ref[...] = held_ref[core]
    send_ref[...] = held_ref[1 - core]


def backward_kernel(
    first_ref, dpre_ref, normed_ref, inv_ref, turned_ref, gain_ref,
    grad_hbm, edge_hbm, same_hbm, other_hbm,
    total_ref, low_ref, grad_ref, edge_ref, rim_ref, done,
):
    cells, width = low_ref.shape
    blocks = cells // HALO
    gain = gain_ref[...]
    inverse = 1.0 / gain
    core = lax.axis_index("co")
    saves = [
        pltpu.make_async_copy(source, place, done.at[i])
        for i, (source, place) in enumerate(
            [
                (rim_ref.at[0], same_hbm),
                (rim_ref.at[1], other_hbm),
                (edge_ref, edge_hbm),
                (grad_ref, grad_hbm.at[HALO : cells - HALO]),
            ]
        )
    ]
    cols = 256
    mean = jnp.zeros((cells, 1), F32)
    along = jnp.zeros((cells, 1), F32)
    for n in range(0, width, cols):
        part = slice(n, n + cols)
        d_normed = dot(dpre_ref[...], first_ref[part, :], 1, 1)
        total_ref[:, part] = d_normed
        mean = mean + jnp.sum(d_normed * gain[:, part], -1, keepdims=True)
        along = along + jnp.sum(d_normed * normed_ref[:, part].astype(F32), -1, keepdims=True)
    for block in range(blocks):
        own = slice(block * HALO, (block + 1) * HALO)
        inner = mean[own] * (1.0 / width) + normed_ref[own, :].astype(F32) * inverse * (
            along[own] * (1.0 / width)
        )
        d_summed = inv_ref[own, :1] * (total_ref[own, :] * gain - inner)
        total_ref[own, :] = d_summed
        low_ref[own, :] = d_summed.astype(BF16)
    for row in (0, blocks + 1, 1, blocks, *range(2, blocks)):
        near = slice(max(row - 2, 0) * HALO, min(row + 1, blocks) * HALO)
        back = dot(turned_ref[row * HALO : (row + 1) * HALO, near], low_ref[near, :]) * (1.0 / NEIGH)
        if row in (0, blocks + 1):
            rim_ref[1 - core if row == 0 else core] = back.astype(BF16)
            if row > 0:
                saves[0].start()
                saves[1].start()
            continue
        value = total_ref[(row - 1) * HALO : row * HALO, :] + back
        if row in (1, blocks):
            edge_ref[0 if row == 1 else 1] = value
        else:
            grad_ref[(row - 2) * HALO : (row - 1) * HALO, :] = value.astype(BF16)
        if row == blocks:
            saves[2].start()
    saves[3].start()
    for save in saves:
        save.wait()


def pair_kernel(fields, keep_ref, got_ref, out_ref):
    last = keep_ref.shape[1] - 1
    for k in range(keep_ref.shape[0]):
        total = keep_ref[k, :last].astype(F32) + got_ref[k, :last].astype(F32)
        out_ref[k, :last] = total.astype(BF16)
        tile = keep_ref[k, last].astype(F32) + got_ref[k, last].astype(F32)
        out_ref[k, last] = split_loss(tile, read_loss(tile, fields), fields).astype(BF16)


def plane_kernel(fields, parts_ref, out_ref):
    me = lax.axis_index("xh") * lax.axis_size("y") + lax.axis_index("y")
    blocks = parts_ref.shape[1] - 1
    for j in range(blocks + 1):
        total = parts_ref[0, j].astype(F32)
        for k in range(1, parts_ref.shape[0]):
            total = total + parts_ref[k, j].astype(F32)
        if j < blocks:
            out_ref[j, 0] = total.astype(BF16)
    loss = read_loss(total, fields)
    for j in range(blocks):
        tile = jnp.where(me == j, total, 0.0)
        out_ref[j, 1] = split_loss(tile, loss, fields).astype(BF16)


def fold_kernel(fields, parts_ref, out_ref):
    total = parts_ref[0].astype(F32)
    for k in range(1, parts_ref.shape[0]):
        total = total + parts_ref[k].astype(F32)
    first = total[0].astype(BF16)
    second = split_loss(total[1], read_loss(total[1], fields), fields).astype(BF16)
    for m in range(out_ref.shape[0]):
        out_ref[m, 0] = first
        out_ref[m, 1] = second


def last_kernel(fields, patches, parts_ref, first_ref, second_ref, loss_ref):
    for k in range(parts_ref.shape[0]):
        first_ref[:, k * LANES : (k + 1) * LANES] = parts_ref[k, 0].astype(F32)
    tile = parts_ref[lax.axis_index("z"), 1].astype(F32)
    second_ref[...] = tile[:, :fields]
    loss_ref[...] = read_loss(tile, fields)[:1, :] * (1.0 / patches)


def edge_kernel(grad_in_ref, edge_ref, same_ref, other_ref, grad_ref):
    del grad_in_ref
    rim = jnp.where(pl.program_id(0) == lax.axis_index("co"), other_ref[...], same_ref[...])
    grad_ref[...] = (edge_ref[0] + rim.astype(F32)).astype(BF16)


BAND = ("z", "xl", "co")
MEM = ("xh", "y")
PLANE = ("y", "xh", "xl")


def per_device(hidden, gain, w_first, w_second, target, patch_ids, neighbours):
    states = hidden[0]
    cells, width = states.shape
    fields = w_second.shape[1]
    bands, members = lax.axis_size(BAND), lax.axis_size(MEM)
    share = width // bands
    chips = [(i, i + 1) for i in range(1, bands - 1, 2)]
    chips = chips + [(j, i) for i, j in chips]
    cores = [(0, 1), (1, 0)]
    rim_same, rim_other = call(
        rims_kernel,
        [shape((HALO, width), BF16), shape((HALO, width), BF16)],
        [states],
        0,
        4,
        [pltpu.SemaphoreType.DMA((2,))],
        anywhere=(0,),
        held=(0, 1),
    )
    other = lax.ppermute(rim_other, BAND, chips)
    same = lax.ppermute(rim_same, "co", cores)
    half = cells // 2
    saved = [shape((half, width), BF16)] * 3 + [shape((half, LANES), F32)]
    *inside, gain, first, second, partial, outside, turned = call(
        inner_kernel,
        [
            shape((fields, half), BF16),
            *saved,
            shape((1, width), F32),
            shape(w_first.shape, BF16),
            shape((fields, width), BF16),
            shape((half, width), F32),
            shape((2, HALO, HALO), BF16),
            shape((cells + 2 * HALO, cells), BF16),
        ],
        [neighbours, states, gain[None], w_first, w_second.T],
        10**9,
        16,
        [
            pltpu.VMEM(neighbours.shape, jnp.int32),
            pltpu.VMEM(states.shape, BF16),
            pltpu.SemaphoreType.DMA((5,)),
        ],
        anywhere=(0, 1, 2, 3, 4),
        held=(5, 6, 7),
    )
    saved = [shape((cells, width), BF16)] * 3 + [shape((cells, LANES), F32)]
    copies, slope, active, normed, inv_root = call(
        outer_kernel,
        [shape((members, fields, cells), BF16)] + saved,
        [same, other, partial, outside, gain, second, *inside, first],
        10**9,
        20,
        [pltpu.VMEM((half, width), BF16)],
    )
    everyone = lax.all_to_all(copies, MEM, 0, 0)
    message = (2 * members, members + 1, share, LANES)
    keep, send, d_pre = call(
        score_kernel,
        [shape(message, BF16), shape(message, BF16), shape((cells, width), BF16)],
        [everyone, target, patch_ids[None], second, slope, active, normed],
        2 * 10**9,
        20,
        [pltpu.VMEM((2,) + message, BF16)],
    )
    got = lax.ppermute(send, "co", cores)
    grad, edge, rim_same, rim_other = call(
        backward_kernel,
        [
            shape((cells, width), BF16),
            shape((2, HALO, width), F32),
            shape((HALO, width), BF16),
            shape((HALO, width), BF16),
        ],
        [first, d_pre, normed, inv_root, turned, gain],
        2 * 10**9,
        20,
        [
            pltpu.VMEM((cells, width), F32),
            pltpu.VMEM((cells, width), BF16),
            pltpu.VMEM((cells - 2 * HALO, width), BF16),
            pltpu.VMEM((2, HALO, width), F32),
            pltpu.VMEM((2, HALO, width), BF16),
            pltpu.SemaphoreType.DMA((4,)),
        ],
        stored=(0, 1, 2, 3),
    )
    got, grad = lax.optimization_barrier((got, grad))
    (mine,) = call(
        functools.partial(pair_kernel, fields), [shape(message, BF16)], [keep, got], 10**6, 8
    )
    parts = lax.all_to_all(mine, PLANE, 0, 0)
    parts, rim_same, rim_other = lax.optimization_barrier((parts, rim_same, rim_other))
    other = lax.ppermute(rim_other, BAND, chips)
    same = lax.ppermute(rim_same, "co", cores)
    last = cells // HALO - 1
    grad_hidden = pl.pallas_call(
        edge_kernel,
        grid=(2,),
        out_shape=shape((cells, width), BF16),
        in_specs=[
            pl.BlockSpec(memory_space=pl.ANY),
            pl.BlockSpec((1, HALO, width), lambda i: (i, 0, 0)),
            pl.BlockSpec((HALO, width), lambda i: (0, 0)),
            pl.BlockSpec((HALO, width), lambda i: (0, 0)),
        ],
        out_specs=pl.BlockSpec((HALO, width), lambda i: (i * last, 0)),
        input_output_aliases={0: 0},
        compiler_params=pltpu.CompilerParams(vmem_limit_bytes=8 * 2**20),
    )(grad, edge, same, other)
    message = (members, 2, share, LANES)
    (planed,) = call(
        functools.partial(plane_kernel, fields), [shape(message, BF16)], [parts], 10**6, 8
    )
    parts = lax.all_to_all(planed, "z", 0, 0)
    (folded,) = call(
        functools.partial(fold_kernel, fields), [shape(message, BF16)], [parts], 10**6, 8
    )
    parts = lax.all_to_all(folded, MEM, 0, 0)
    grad_first, grad_second, loss = call(
        functools.partial(last_kernel, fields, cells // PATCH * bands),
        [shape((share, width), F32), shape((share, fields), F32), shape((1, 1), F32)],
        [parts],
        10**6,
        8,
    )
    return (loss[0, 0], grad_hidden[None], grad_first, grad_second)


def solution(mesh):
    split = jax.sharding.Mesh(mesh.devices.reshape(8, 2, 2, 2, 4), BAND + MEM)
    return jax.shard_map(
        per_device,
        mesh=split,
        in_specs=(
            P(MEM, BAND, None),
            P(),
            P(),
            P(),
            P(None, BAND),
            P(BAND),
            P(None, BAND),
        ),
        out_specs=(P(), P(MEM, BAND, None), P(BAND, None), P(BAND, None)),
        check_vma=False,
    )
```

```python
import functools
import math

import jax
import jax.numpy as jnp
from jax import lax
from jax.experimental import pallas as pl
from jax.experimental.pallas import tpu as pltpu
from jax.sharding import PartitionSpec as P

PATCH = 256
NEIGH = 6
HALO = 128
EPS_NORM = 1e-05
EPS_DIST = 1e-06
LANES = 128
F32 = jnp.float32
BF16 = jnp.bfloat16
VMEM = pl.BlockSpec(memory_space=pltpu.VMEM)
ANY = pl.BlockSpec(memory_space=pl.ANY)


def dot(a, b, ca=1, cb=0):
    return lax.dot_general(a, b, (((ca,), (cb,)), ((), ())), preferred_element_type=F32)


def call(kernel, outs, args, flops, limit, scratch=(), anywhere=(), stored=(), held=()):
    args = [
        pltpu.with_memory_space_constraint(a, pltpu.HBM) if i in anywhere else a
        for i, a in enumerate(args)
    ]
    moved = sum(math.prod(a.shape) * a.dtype.itemsize for a in list(args) + list(outs))
    return pl.pallas_call(
        kernel,
        out_shape=[
            pltpu.HBM(o.shape, o.dtype) if i in stored else pltpu.VMEM(o.shape, o.dtype) if i in held else o
            for i, o in enumerate(outs)
        ],
        in_specs=[ANY if i in anywhere else VMEM for i in range(len(args))],
        out_specs=[ANY if i in stored else VMEM for i in range(len(outs))],
        scratch_shapes=list(scratch),
        compiler_params=pltpu.CompilerParams(vmem_limit_bytes=limit * 2**20),
        cost_estimate=pl.CostEstimate(flops=flops, bytes_accessed=moved, transcendentals=0),
    )(*args)


def shape(dims, kind):
    return jax.ShapeDtypeStruct(dims, kind)


def rims_kernel(states_hbm, same_ref, other_ref, done):
    rows = states_hbm.shape[0]
    core = lax.axis_index("co")
    low, high = core * (rows - HALO), (1 - core) * (rows - HALO)
    moves = [
        pltpu.make_async_copy(states_hbm.at[pl.ds(low, HALO)], other_ref, done.at[0]),
        pltpu.make_async_copy(states_hbm.at[pl.ds(high, HALO)], same_ref, done.at[1]),
    ]
    for move in moves:
        move.start()
    for move in moves:
        move.wait()


def count_rows(near, block):
    near = near[:, block * HALO : (block + 1) * HALO]
    row = lax.broadcasted_iota(jnp.int32, (3 * HALO, HALO), 0)
    own = lax.broadcasted_iota(jnp.int32, (3 * HALO, HALO), 1) + HALO
    total = jnp.where(row == own, float(NEIGH), 0.0)
    for k in range(NEIGH):
        total = total + jnp.where(near[k : k + 1, :] == row + block * HALO, 1.0, 0.0)
    return total


def normalise(summed, gain):
    centred = summed - jnp.mean(summed, -1, keepdims=True)
    inv_root = lax.rsqrt(jnp.mean(centred * centred, -1, keepdims=True) + EPS_NORM)
    normed = (centred * inv_root * gain).astype(BF16)
    return normed, jnp.broadcast_to(inv_root, (summed.shape[0], LANES))


def head(normed_ref, first_ref, part):
    preact = dot(normed_ref[...], first_ref[:, part])
    share = 0.5 * (1.0 + lax.erf(preact * math.sqrt(0.5)))
    bell = jnp.exp(-0.5 * preact * preact) * (1.0 / math.sqrt(2.0 * math.pi))
    return (preact * share).astype(BF16), (share + preact * bell).astype(BF16)


def inner_kernel(
    same_ref, near_hbm, states_hbm, gain_hbm, first_hbm, second_hbm,
    predicted_ref, slope_ref, active_ref, normed_ref, inv_ref, gain_ref, first_ref, second_ref,
    partial_ref, outside_ref, turned_ref, first_turned_ref,
    near_ref, states_ref, done,
):
    loads = [
        pltpu.make_async_copy(source, place, done.at[i])
        for i, (source, place) in enumerate(
            [
                (near_hbm, near_ref),
                (states_hbm, states_ref),
                (gain_hbm, gain_ref),
                (first_hbm, first_ref),
                (second_hbm, second_ref),
            ]
        )
    ]
    for load in loads:
        load.start()
    core = lax.axis_index("co")
    loads[0].wait()
    near = near_ref[...]
    cells = states_ref.shape[0]
    blocks = cells // HALO
    counts = []
    for block in range(blocks):
        total = count_rows(near, block)
        turned_ref[block * HALO : (block + 3) * HALO, block * HALO : (block + 1) * HALO] = total.astype(BF16)
        counts.append(total.T.astype(BF16))
    outside = (counts[0][:, :HALO], counts[-1][:, 2 * HALO :])
    inside = (counts[0][:, HALO:], counts[-1][:, : 2 * HALO])
    loads[1].wait()
    loads[2].wait()
    gain = gain_ref[...]
    for block in range(1, blocks - 1):
        reach = states_ref[(block - 1) * HALO : (block + 2) * HALO, :]
        summed = dot(counts[block], reach) * (1.0 / NEIGH)
        to = slice((block - 1) * HALO, block * HALO)
        normed_ref[to, :], inv_ref[to, :] = normalise(summed, gain)
    last = cells - 2 * HALO
    rows = states_ref[pl.ds(pl.multiple_of((1 - core) * last, HALO), 2 * HALO), :]
    summed = dot(jnp.where(core == 0, inside[1], inside[0]), rows)
    summed = summed + dot(jnp.where(core == 0, outside[1], outside[0]), same_ref[...])
    normed_ref[last:, :], inv_ref[last:, :] = normalise(summed * (1.0 / NEIGH), gain)
    rows = states_ref[pl.ds(pl.multiple_of(core * last, HALO), 2 * HALO), :]
    partial_ref[...] = dot(jnp.where(core == 0, inside[0], inside[1]), rows)
    outside_ref[...] = jnp.where(core == 0, outside[0], outside[1])
    loads[3].wait()
    loads[4].wait()
    cols = 256
    for n in range(0, normed_ref.shape[1], cols):
        part = slice(n, n + cols)
        active_ref[:, part], slope_ref[:, part] = head(normed_ref, first_ref, part)
    predicted_ref[...] = dot(second_ref[...], active_ref[...], 1, 1).astype(BF16)
    for n in range(0, first_ref.shape[0], LANES):
        first_turned_ref[:, n : n + LANES] = first_ref[n : n + LANES, :].T


def outer_kernel(
    other_ref, partial_ref, outside_ref, gain_ref, second_ref,
    predicted_in_ref, slope_in_ref, active_in_ref, normed_in_ref, inv_in_ref, first_ref,
    copies_ref, slope_ref, active_ref, normed_ref, inv_ref,
    own_ref,
):
    cells, width = normed_ref.shape
    core = lax.axis_index("co")
    last = cells - HALO
    inner, held = slice(HALO, last), slice(0, last - HALO)
    mine = pl.ds(pl.multiple_of(core * last, HALO), HALO)
    done = pl.ds(pl.multiple_of((1 - core) * last, HALO), HALO)
    summed = (partial_ref[...] + dot(outside_ref[...], other_ref[...])) * (1.0 / NEIGH)
    normed, inv_ref[mine, :] = normalise(summed, gain_ref[...])
    normed_ref[mine, :] = normed
    own_ref[...] = normed
    for full_ref, part_ref in (
        (normed_ref, normed_in_ref),
        (inv_ref, inv_in_ref),
        (active_ref, active_in_ref),
        (slope_ref, slope_in_ref),
    ):
        full_ref[inner, :] = part_ref[held, :]
        full_ref[done, :] = part_ref[last - HALO :, :]
    cols = 256
    for n in range(0, width, cols):
        part = slice(n, n + cols)
        active_ref[mine, part], slope_ref[mine, part] = head(own_ref, first_ref, part)
    predicted = dot(second_ref[...], active_ref[mine, :], 1, 1).astype(BF16)
    for m in range(copies_ref.shape[0]):
        copies_ref[m, :, inner] = predicted_in_ref[:, held]
        copies_ref[m, :, done] = predicted_in_ref[:, last - HALO :]
        copies_ref[m, :, mine] = predicted


def split_loss(tile, loss, fields):
    lane = lax.broadcasted_iota(jnp.int32, tile.shape, 1)
    high = loss.astype(BF16).astype(F32)
    low = loss - high
    return jnp.where(lane == fields, high, jnp.where(lane == fields + 1, low, tile))


def read_loss(tile, fields):
    lane = lax.broadcasted_iota(jnp.int32, tile.shape, 1)
    here = (lane == fields) | (lane == fields + 1)
    return jnp.sum(jnp.where(here, tile, 0.0), axis=1, keepdims=True)


def score_kernel(
    everyone_ref, target_ref, patch_ref, second_ref, slope_ref, active_ref, normed_ref,
    keep_ref, send_ref, dpre_ref,
):
    members, fields, cells = everyone_ref.shape
    width = slope_ref.shape[1]
    me = member_place(lax.axis_index("xh") * lax.axis_size("y") + lax.axis_index("y"), members)
    entries = fields * PATCH
    share = keep_ref.shape[2]

    def target_of(xl, member):
        return (member % 4) * 4 + (member // 4) * 2 + xl

    places = [(b, ((b // 2) % 2, b // 4)) for b in range(width // share)]
    own = everyone_ref[me].astype(F32)
    error = own - target_ref[...]
    sums = [jnp.sum(error * error, axis=0, keepdims=True)]
    for n in range(members):
        differ = own - everyone_ref[n].astype(F32)
        sums.append(jnp.sum(differ * differ, axis=0, keepdims=True))
    sums.append(jnp.zeros((16 - len(sums), cells), F32))
    sums = jnp.concatenate(sums, 0)
    even = (patch_ref[...] & 1) == 0
    spread_even = jnp.sqrt(jnp.sum(jnp.where(even, sums, 0.0), 1, keepdims=True) / entries + EPS_DIST)
    spread_odd = jnp.sqrt(jnp.sum(jnp.where(even, 0.0, sums), 1, keepdims=True) / entries + EPS_DIST)
    row = lax.broadcasted_iota(jnp.int32, (16, 1), 0)
    weight = jnp.where(row == 0, 1.0 / members, 1.0 / (members * (members - 1)))
    scale = jnp.where(even, weight / spread_even, weight / spread_odd)
    gradient = error * scale[0:1]
    for n in range(members):
        differ = own - everyone_ref[n].astype(F32)
        gradient = gradient - differ * scale[n + 1 : n + 2]
    both = spread_even + spread_odd
    used = jnp.where(row == 0, 1.0 / members, -0.5 / (members * (members - 1)))
    used = jnp.where((row == me + 1) | (row > members), 0.0, used)
    loss = jnp.sum(both * used, axis=0, keepdims=True)

    gradient = jnp.concatenate([gradient, jnp.zeros((LANES - fields, cells), F32)], 0)
    outer = gradient.T.astype(BF16)
    cols = 256
    for n in range(0, width, cols):
        part = slice(n, n + cols)
        d_active = dot(outer[:, :fields], second_ref[:, part])
        dpre_ref[:, part] = (d_active * slope_ref[:, part].astype(F32)).astype(BF16)

    def weight_grads(kept):
        for n in range(0, width, cols):
            grad = dot(normed_ref[...], dpre_ref[:, n : n + cols], 0, 0).astype(BF16)
            for band, slot in places:
                to_ref = keep_ref if band % 2 == kept else send_ref
                rows = grad[band * share : (band + 1) * share]
                for c in range(0, cols, LANES):
                    to_ref[target_of(slot[0], (n + c) // LANES), slot[1]] = rows[:, c : c + LANES]
        grad = dot(active_ref[...], outer, 0, 0)
        grad = split_loss(grad, loss, fields).astype(BF16)
        for band, slot in places:
            to_ref = keep_ref if band % 2 == kept else send_ref
            to_ref[target_of(slot[0], slot[1]), members] = grad[band * share : (band + 1) * share]

    core = lax.axis_index("co")
    pl.when(core == 0)(lambda: weight_grads(0))
    pl.when(core == 1)(lambda: weight_grads(1))


def backward_kernel(
    first_ref, dpre_ref, normed_ref, inv_ref, turned_ref, gain_ref,
    grad_hbm, edge_hbm, same_hbm, other_hbm,
    total_ref, low_ref, grad_ref, edge_ref, rim_ref, done,
):
    cells, width = low_ref.shape
    blocks = cells // HALO
    gain = gain_ref[...]
    inverse = 1.0 / gain
    core = lax.axis_index("co")
    saves = [
        pltpu.make_async_copy(source, place, done.at[i])
        for i, (source, place) in enumerate(
            [
                (rim_ref.at[0], same_hbm),
                (rim_ref.at[1], other_hbm),
                (edge_ref, edge_hbm),
                *(
                    (grad_ref.at[i : i + HALO], grad_hbm.at[i + HALO : i + 2 * HALO])
                    for i in range(0, cells - 2 * HALO, HALO)
                ),
            ]
        )
    ]
    cols = 256
    mean = jnp.zeros((cells, LANES), F32)
    along = jnp.zeros((cells, LANES), F32)
    for n in range(0, width, cols):
        part = slice(n, n + cols)
        d_normed = dot(dpre_ref[...], first_ref[:, part])
        scaled = d_normed * gain[:, part]
        total_ref[:, part] = scaled
        shared = d_normed * normed_ref[:, part].astype(F32)
        for c in range(0, cols, LANES):
            mean = mean + scaled[:, c : c + LANES]
            along = along + shared[:, c : c + LANES]
    mean = jnp.sum(mean, -1, keepdims=True)
    along = jnp.sum(along, -1, keepdims=True)
    for block in range(blocks):
        own = slice(block * HALO, (block + 1) * HALO)
        inner = mean[own] * (1.0 / width) + normed_ref[own, :].astype(F32) * inverse * (
            along[own] * (1.0 / width)
        )
        low_ref[own, :] = (inv_ref[own, :1] * (total_ref[own, :] - inner)).astype(BF16)
    for row in (0, blocks + 1, 1, blocks, *range(2, blocks)):
        near = slice(max(row - 2, 0) * HALO, min(row + 1, blocks) * HALO)
        back = dot(turned_ref[row * HALO : (row + 1) * HALO, near], low_ref[near, :]) * (1.0 / NEIGH)
        if row in (0, blocks + 1):
            rim_ref[1 - core if row == 0 else core] = back.astype(BF16)
            if row > 0:
                saves[0].start()
                saves[1].start()
            continue
        if row in (1, blocks):
            edge_ref[0 if row == 1 else 1] = back
        else:
            grad_ref[(row - 2) * HALO : (row - 1) * HALO, :] = back.astype(BF16)
            saves[row + 1].start()
        if row == blocks:
            saves[2].start()
    for save in saves:
        save.wait()


def pair_kernel(fields, keep_ref, got_ref, out_ref):
    last = keep_ref.shape[1] - 1
    for k in range(keep_ref.shape[0]):
        total = keep_ref[k, :last].astype(F32) + got_ref[k, :last].astype(F32)
        out_ref[k, :last] = total.astype(BF16)
        tile = keep_ref[k, last].astype(F32) + got_ref[k, last].astype(F32)
        out_ref[k, last] = split_loss(tile, read_loss(tile, fields), fields).astype(BF16)


def plane_kernel(fields, parts_ref, out_ref):
    me = lax.axis_index("xh") * lax.axis_size("y") + lax.axis_index("y")
    blocks = parts_ref.shape[1] - 1
    for j in range(blocks + 1):
        total = parts_ref[0, j].astype(F32)
        for k in range(1, parts_ref.shape[0]):
            total = total + parts_ref[k, j].astype(F32)
        if j < blocks:
            out_ref[j, 0] = total.astype(BF16)
    loss = read_loss(total, fields)
    for j in range(blocks):
        tile = jnp.where(me == j, total, 0.0)
        out_ref[j, 1] = split_loss(tile, loss, fields).astype(BF16)


def fold_kernel(fields, parts_ref, out_ref):
    total = parts_ref[0].astype(F32)
    for k in range(1, parts_ref.shape[0]):
        total = total + parts_ref[k].astype(F32)
    first = total[0].astype(BF16)
    second = split_loss(total[1], read_loss(total[1], fields), fields).astype(BF16)
    for m in range(out_ref.shape[0]):
        out_ref[m, 0] = first
        out_ref[m, 1] = second


def last_kernel(fields, patches, parts_ref, first_ref, second_ref, loss_ref):
    members = parts_ref.shape[0]
    for m in range(members):
        first_ref[:, m * LANES : (m + 1) * LANES] = parts_ref[member_place(m, members), 0].astype(F32)
    tile = parts_ref[member_place(lax.axis_index("z"), members), 1].astype(F32)
    second_ref[...] = tile[:, :fields]
    loss_ref[...] = read_loss(tile, fields)[:1, :] * (1.0 / patches)


def edge_kernel(grad_in_ref, edge_ref, same_ref, other_ref, grad_ref):
    del grad_in_ref
    rim = jnp.where(pl.program_id(0) == lax.axis_index("co"), other_ref[...], same_ref[...])
    grad_ref[...] = (edge_ref[0] + rim.astype(F32)).astype(BF16)


BAND = ("z", "xl", "co")
MEM = ("xh", "y")
PLANE = ("y", "xh", "xl")


def member_groups(bands, members):
    groups = []
    for band in range(bands):
        group = [band * members + m for m in range(members)]
        groups.append(group if band % 2 == 0 else group[::-1])
    return groups


def member_place(member, members):
    return jnp.where(lax.axis_index("co") == 0, member, members - 1 - member)


def per_device(hidden, gain, w_first, w_second, target, patch_ids, neighbours):
    states = hidden[0]
    cells, width = states.shape
    fields = w_second.shape[1]
    bands, members = lax.axis_size(BAND), lax.axis_size(MEM)
    share = width // bands
    chips = [(i, i + 1) for i in range(1, bands - 1, 2)]
    chips = chips + [(j, i) for i, j in chips]
    cores = [(0, 1), (1, 0)]
    rim_same, rim_other = call(
        rims_kernel,
        [shape((HALO, width), BF16), shape((HALO, width), BF16)],
        [states],
        0,
        4,
        [pltpu.SemaphoreType.DMA((2,))],
        anywhere=(0,),
        held=(0, 1),
    )
    same = lax.ppermute(rim_same, "co", cores)
    other = lax.ppermute(rim_other, BAND, chips)
    held = cells - HALO
    saved = [shape((held, width), BF16)] * 3 + [shape((held, LANES), F32)]
    *inside, gain, first, second, partial, outside, turned, first_turned = call(
        inner_kernel,
        [
            shape((fields, held), BF16),
            *saved,
            shape((1, width), F32),
            shape(w_first.shape, BF16),
            shape((fields, width), BF16),
            shape((HALO, width), F32),
            shape((HALO, HALO), BF16),
            shape((cells + 2 * HALO, cells), BF16),
            shape(w_first.shape[::-1], BF16),
        ],
        [same, neighbours, states, gain[None], w_first, w_second.T],
        10**9,
        16,
        [
            pltpu.VMEM(neighbours.shape, jnp.int32),
            pltpu.VMEM(states.shape, BF16),
            pltpu.SemaphoreType.DMA((5,)),
        ],
        anywhere=(1, 2, 3, 4, 5),
        held=(5, 6, 7, 10, 11),
    )
    saved = [shape((cells, width), BF16)] * 3 + [shape((cells, LANES), F32)]
    copies, slope, active, normed, inv_root = call(
        outer_kernel,
        [shape((members, fields, cells), BF16)] + saved,
        [other, partial, outside, gain, second, *inside, first],
        10**9,
        20,
        [pltpu.VMEM((HALO, width), BF16)],
    )
    groups = member_groups(bands, members)
    everyone = lax.all_to_all(copies, BAND + MEM, 0, 0, axis_index_groups=groups)
    message = (2 * members, members + 1, share, LANES)
    keep, send, d_pre = call(
        score_kernel,
        [shape(message, BF16), shape(message, BF16), shape((cells, width), BF16)],
        [everyone, target, patch_ids[None], second, slope, active, normed],
        2 * 10**9,
        20,
    )
    got = lax.ppermute(send, "co", cores)
    grad, edge, rim_same, rim_other = call(
        backward_kernel,
        [
            shape((cells, width), BF16),
            shape((2, HALO, width), F32),
            shape((HALO, width), BF16),
            shape((HALO, width), BF16),
        ],
        [first_turned, d_pre, normed, inv_root, turned, gain],
        2 * 10**9,
        20,
        [
            pltpu.VMEM((cells, width), F32),
            pltpu.VMEM((cells, width), BF16),
            pltpu.VMEM((cells - 2 * HALO, width), BF16),
            pltpu.VMEM((2, HALO, width), F32),
            pltpu.VMEM((2, HALO, width), BF16),
            pltpu.SemaphoreType.DMA((3 + cells // HALO - 2,)),
        ],
        stored=(0, 1, 2, 3),
    )
    got, grad = lax.optimization_barrier((got, grad))
    (mine,) = call(
        functools.partial(pair_kernel, fields), [shape(message, BF16)], [keep, got], 10**6, 8
    )
    parts = lax.all_to_all(mine, PLANE, 0, 0)
    parts, rim_same, rim_other = lax.optimization_barrier((parts, rim_same, rim_other))
    same = lax.ppermute(rim_same, "co", cores)
    other = lax.ppermute(rim_other, BAND, chips)
    last = cells // HALO - 1
    grad_hidden = pl.pallas_call(
        edge_kernel,
        grid=(2,),
        out_shape=shape((cells, width), BF16),
        in_specs=[
            pl.BlockSpec(memory_space=pl.ANY),
            pl.BlockSpec((1, HALO, width), lambda i: (i, 0, 0)),
            pl.BlockSpec((HALO, width), lambda i: (0, 0)),
            pl.BlockSpec((HALO, width), lambda i: (0, 0)),
        ],
        out_specs=pl.BlockSpec((HALO, width), lambda i: (i * last, 0)),
        input_output_aliases={0: 0},
        compiler_params=pltpu.CompilerParams(vmem_limit_bytes=8 * 2**20),
    )(grad, edge, same, other)
    message = (members, 2, share, LANES)
    (planed,) = call(
        functools.partial(plane_kernel, fields), [shape(message, BF16)], [parts], 10**6, 8
    )
    parts = lax.all_to_all(planed, "z", 0, 0)
    (folded,) = call(
        functools.partial(fold_kernel, fields), [shape(message, BF16)], [parts], 10**6, 8
    )
    parts = lax.all_to_all(folded, BAND + MEM, 0, 0, axis_index_groups=groups)
    grad_first, grad_second, loss = call(
        functools.partial(last_kernel, fields, cells // PATCH * bands),
        [shape((share, width), F32), shape((share, fields), F32), shape((1, 1), F32)],
        [parts],
        10**6,
        8,
    )
    return (loss[0, 0], grad_hidden[None], grad_first, grad_second)


def solution(mesh):
    split = jax.sharding.Mesh(mesh.devices.reshape(8, 2, 2, 2, 4), BAND + MEM)
    return jax.shard_map(
        per_device,
        mesh=split,
        in_specs=(
            P(MEM, BAND, None),
            P(),
            P(),
            P(),
            P(None, BAND),
            P(BAND),
            P(None, BAND),
        ),
        out_specs=(P(), P(MEM, BAND, None), P(BAND, None), P(BAND, None)),
        check_vma=False,
    )
```

```python
import functools
import math

import jax
import jax.numpy as jnp
from jax import lax
from jax.experimental import pallas as pl
from jax.experimental.pallas import tpu as pltpu
from jax.sharding import PartitionSpec as P

PATCH = 256
NEIGH = 6
HALO = 128
EPS_NORM = 1e-05
EPS_DIST = 1e-06
LANES = 128
F32 = jnp.float32
BF16 = jnp.bfloat16
VMEM = pl.BlockSpec(memory_space=pltpu.VMEM)
ANY = pl.BlockSpec(memory_space=pl.ANY)


def dot(a, b, ca=1, cb=0):
    return lax.dot_general(a, b, (((ca,), (cb,)), ((), ())), preferred_element_type=F32)


def call(kernel, outs, args, flops, limit, scratch=(), anywhere=(), stored=(), held=()):
    args = [
        pltpu.with_memory_space_constraint(a, pltpu.HBM) if i in anywhere else a
        for i, a in enumerate(args)
    ]
    moved = sum(math.prod(a.shape) * a.dtype.itemsize for a in list(args) + list(outs))
    return pl.pallas_call(
        kernel,
        out_shape=[
            pltpu.HBM(o.shape, o.dtype) if i in stored else pltpu.VMEM(o.shape, o.dtype) if i in held else o
            for i, o in enumerate(outs)
        ],
        in_specs=[ANY if i in anywhere else VMEM for i in range(len(args))],
        out_specs=[ANY if i in stored else VMEM for i in range(len(outs))],
        scratch_shapes=list(scratch),
        compiler_params=pltpu.CompilerParams(vmem_limit_bytes=limit * 2**20),
        cost_estimate=pl.CostEstimate(flops=flops, bytes_accessed=moved, transcendentals=0)
        if flops
        else None,
    )(*args)


def shape(dims, kind):
    return jax.ShapeDtypeStruct(dims, kind)


def rims_kernel(states_hbm, same_ref, other_ref, done):
    rows = states_hbm.shape[0]
    core = lax.axis_index("co")
    low, high = core * (rows - HALO), (1 - core) * (rows - HALO)
    moves = [
        pltpu.make_async_copy(states_hbm.at[pl.ds(low, HALO)], other_ref, done.at[0]),
        pltpu.make_async_copy(states_hbm.at[pl.ds(high, HALO)], same_ref, done.at[1]),
    ]
    for move in moves:
        move.start()
    for move in moves:
        move.wait()


def count_rows(near, block):
    near = near[:, block * HALO : (block + 1) * HALO]
    row = lax.broadcasted_iota(jnp.int32, (3 * HALO, HALO), 0)
    own = lax.broadcasted_iota(jnp.int32, (3 * HALO, HALO), 1) + HALO
    total = jnp.where(row == own, float(NEIGH), 0.0)
    for k in range(NEIGH):
        total = total + jnp.where(near[k : k + 1, :] == row + block * HALO, 1.0, 0.0)
    return total


def normalise(summed, gain):
    centred = summed - jnp.mean(summed, -1, keepdims=True)
    inv_root = lax.rsqrt(jnp.mean(centred * centred, -1, keepdims=True) + EPS_NORM)
    normed = (centred * inv_root * gain).astype(BF16)
    return normed, jnp.broadcast_to(inv_root, (summed.shape[0], LANES))


def head(normed_ref, first_ref, part):
    preact = dot(normed_ref[...], first_ref[:, part])
    share = 0.5 * (1.0 + lax.erf(preact * math.sqrt(0.5)))
    bell = jnp.exp(-0.5 * preact * preact) * (1.0 / math.sqrt(2.0 * math.pi))
    return (preact * share).astype(BF16), (share + preact * bell).astype(BF16)


def inner_kernel(
    same_ref, near_hbm, states_hbm, gain_hbm, first_hbm, second_hbm,
    predicted_ref, slope_ref, active_ref, normed_ref, inv_ref, gain_ref, first_ref, second_ref,
    partial_ref, outside_ref, turned_ref, first_turned_ref, turned_hbm,
    near_ref, states_ref, done,
):
    loads = [
        pltpu.make_async_copy(source, place, done.at[i])
        for i, (source, place) in enumerate(
            [
                (near_hbm, near_ref),
                (states_hbm, states_ref),
                (gain_hbm, gain_ref),
                (first_hbm, first_ref),
                (second_hbm, second_ref),
            ]
        )
    ]
    for load in loads:
        load.start()
    core = lax.axis_index("co")
    loads[0].wait()
    near = near_ref[...]
    cells = states_ref.shape[0]
    blocks = cells // HALO
    counts = []
    for block in range(blocks):
        total = count_rows(near, block)
        turned_ref[block * HALO : (block + 3) * HALO, block * HALO : (block + 1) * HALO] = total.astype(BF16)
        counts.append(total.T.astype(BF16))
    save = pltpu.make_async_copy(turned_ref, turned_hbm, done.at[5])
    save.start()
    outside = (counts[0][:, :HALO], counts[-1][:, 2 * HALO :])
    inside = (counts[0][:, HALO:], counts[-1][:, : 2 * HALO])
    loads[1].wait()
    loads[2].wait()
    gain = gain_ref[...]
    for block in range(1, blocks - 1):
        reach = states_ref[(block - 1) * HALO : (block + 2) * HALO, :]
        summed = dot(counts[block], reach) * (1.0 / NEIGH)
        to = slice((block - 1) * HALO, block * HALO)
        normed_ref[to, :], inv_ref[to, :] = normalise(summed, gain)
    last = cells - 2 * HALO
    rows = states_ref[pl.ds(pl.multiple_of((1 - core) * last, HALO), 2 * HALO), :]
    summed = dot(jnp.where(core == 0, inside[1], inside[0]), rows)
    summed = summed + dot(jnp.where(core == 0, outside[1], outside[0]), same_ref[...])
    normed_ref[last:, :], inv_ref[last:, :] = normalise(summed * (1.0 / NEIGH), gain)
    rows = states_ref[pl.ds(pl.multiple_of(core * last, HALO), 2 * HALO), :]
    partial_ref[...] = dot(jnp.where(core == 0, inside[0], inside[1]), rows)
    outside_ref[...] = jnp.where(core == 0, outside[0], outside[1])
    loads[3].wait()
    loads[4].wait()
    cols = 256
    for n in range(0, normed_ref.shape[1], cols):
        part = slice(n, n + cols)
        active_ref[:, part], slope_ref[:, part] = head(normed_ref, first_ref, part)
    predicted_ref[...] = dot(second_ref[...], active_ref[...], 1, 1).astype(BF16)
    for n in range(0, first_ref.shape[0], LANES):
        first_turned_ref[:, n : n + LANES] = first_ref[n : n + LANES, :].T
    save.wait()


def outer_kernel(
    other_ref, partial_ref, outside_ref, gain_ref, second_ref,
    predicted_in_ref, slope_in_ref, active_in_ref, normed_in_ref, inv_in_ref, first_ref,
    copies_ref, slope_ref, active_ref, normed_ref, inv_ref,
    own_ref,
):
    cells, width = normed_ref.shape
    core = lax.axis_index("co")
    last = cells - HALO
    inner, held = slice(HALO, last), slice(0, last - HALO)
    mine = pl.ds(pl.multiple_of(core * last, HALO), HALO)
    done = pl.ds(pl.multiple_of((1 - core) * last, HALO), HALO)
    summed = (partial_ref[...] + dot(outside_ref[...], other_ref[...])) * (1.0 / NEIGH)
    normed, inv_ref[mine, :] = normalise(summed, gain_ref[...])
    normed_ref[mine, :] = normed
    own_ref[...] = normed
    for full_ref, part_ref in (
        (normed_ref, normed_in_ref),
        (inv_ref, inv_in_ref),
        (active_ref, active_in_ref),
        (slope_ref, slope_in_ref),
    ):
        full_ref[inner, :] = part_ref[held, :]
        full_ref[done, :] = part_ref[last - HALO :, :]
    cols = 256
    for n in range(0, width, cols):
        part = slice(n, n + cols)
        active_ref[mine, part], slope_ref[mine, part] = head(own_ref, first_ref, part)
    predicted = dot(second_ref[...], active_ref[mine, :], 1, 1).astype(BF16)
    for m in range(copies_ref.shape[0]):
        copies_ref[m, :, inner] = predicted_in_ref[:, held]
        copies_ref[m, :, done] = predicted_in_ref[:, last - HALO :]
        copies_ref[m, :, mine] = predicted


def split_loss(tile, loss, fields):
    lane = lax.broadcasted_iota(jnp.int32, tile.shape, 1)
    high = loss.astype(BF16).astype(F32)
    low = loss - high
    return jnp.where(lane == fields, high, jnp.where(lane == fields + 1, low, tile))


def read_loss(tile, fields):
    lane = lax.broadcasted_iota(jnp.int32, tile.shape, 1)
    here = (lane == fields) | (lane == fields + 1)
    return jnp.sum(jnp.where(here, tile, 0.0), axis=1, keepdims=True)


def score_kernel(
    everyone_ref, target_ref, patch_ref, second_ref, slope_ref, active_ref, normed_ref,
    keep_ref, send_ref, dpre_ref,
):
    members, fields, cells = everyone_ref.shape
    width = slope_ref.shape[1]
    me = member_place(lax.axis_index("xh") * lax.axis_size("y") + lax.axis_index("y"), members)
    entries = fields * PATCH
    share = keep_ref.shape[2]

    def target_of(xl, member):
        return (member % 4) * 4 + (member // 4) * 2 + xl

    places = [(b, ((b // 2) % 2, b // 4)) for b in range(width // share)]
    own = everyone_ref[me].astype(F32)
    error = own - target_ref[...]
    sums = [jnp.sum(error * error, axis=0, keepdims=True)]
    for n in range(members):
        differ = own - everyone_ref[n].astype(F32)
        sums.append(jnp.sum(differ * differ, axis=0, keepdims=True))
    sums.append(jnp.zeros((16 - len(sums), cells), F32))
    sums = jnp.concatenate(sums, 0)
    even = (patch_ref[...] & 1) == 0
    spread_even = jnp.sqrt(jnp.sum(jnp.where(even, sums, 0.0), 1, keepdims=True) / entries + EPS_DIST)
    spread_odd = jnp.sqrt(jnp.sum(jnp.where(even, 0.0, sums), 1, keepdims=True) / entries + EPS_DIST)
    row = lax.broadcasted_iota(jnp.int32, (16, 1), 0)
    weight = jnp.where(row == 0, 1.0 / members, 1.0 / (members * (members - 1)))
    scale = jnp.where(even, weight / spread_even, weight / spread_odd)
    gradient = error * scale[0:1]
    for n in range(members):
        differ = own - everyone_ref[n].astype(F32)
        gradient = gradient - differ * scale[n + 1 : n + 2]
    both = spread_even + spread_odd
    used = jnp.where(row == 0, 1.0 / members, -0.5 / (members * (members - 1)))
    used = jnp.where((row == me + 1) | (row > members), 0.0, used)
    loss = jnp.sum(both * used, axis=0, keepdims=True)

    gradient = jnp.concatenate([gradient, jnp.zeros((LANES - fields, cells), F32)], 0)
    outer = gradient.T.astype(BF16)
    cols = 256
    for n in range(0, width, cols):
        part = slice(n, n + cols)
        d_active = dot(outer[:, :fields], second_ref[:, part])
        dpre_ref[:, part] = (d_active * slope_ref[:, part].astype(F32)).astype(BF16)

    def weight_grads(kept):
        for n in range(0, width, cols):
            grad = dot(normed_ref[...], dpre_ref[:, n : n + cols], 0, 0).astype(BF16)
            for band, slot in places:
                to_ref = keep_ref if band % 2 == kept else send_ref
                rows = grad[band * share : (band + 1) * share]
                for c in range(0, cols, LANES):
                    to_ref[target_of(slot[0], (n + c) // LANES), slot[1]] = rows[:, c : c + LANES]
        grad = dot(active_ref[...], outer, 0, 0)
        grad = split_loss(grad, loss, fields).astype(BF16)
        for band, slot in places:
            to_ref = keep_ref if band % 2 == kept else send_ref
            to_ref[target_of(slot[0], slot[1]), members] = grad[band * share : (band + 1) * share]

    core = lax.axis_index("co")
    pl.when(core == 0)(lambda: weight_grads(0))
    pl.when(core == 1)(lambda: weight_grads(1))


def backward_kernel(
    first_ref, dpre_ref, normed_ref, inv_ref, turned_ref, gain_ref,
    low_hbm, same_hbm, other_hbm,
    total_ref, low_ref, rim_ref, done,
):
    cells, width = low_ref.shape
    blocks = cells // HALO
    gain = gain_ref[...]
    inverse = 1.0 / gain
    core = lax.axis_index("co")
    saves = [
        pltpu.make_async_copy(source, place, done.at[i])
        for i, (source, place) in enumerate(
            [
                (rim_ref.at[0], same_hbm),
                (rim_ref.at[1], other_hbm),
                (low_ref, low_hbm),
            ]
        )
    ]
    cols = 256
    mean = jnp.zeros((cells, LANES), F32)
    along = jnp.zeros((cells, LANES), F32)
    for n in range(0, width, cols):
        part = slice(n, n + cols)
        d_normed = dot(dpre_ref[...], first_ref[:, part])
        scaled = d_normed * gain[:, part]
        total_ref[:, part] = scaled
        shared = d_normed * normed_ref[:, part].astype(F32)
        for c in range(0, cols, LANES):
            mean = mean + scaled[:, c : c + LANES]
            along = along + shared[:, c : c + LANES]
    mean = jnp.sum(mean, -1, keepdims=True)
    along = jnp.sum(along, -1, keepdims=True)
    for block in (0, blocks - 1, *range(1, blocks - 1)):
        own = slice(block * HALO, (block + 1) * HALO)
        inner = mean[own] * (1.0 / width) + normed_ref[own, :].astype(F32) * inverse * (
            along[own] * (1.0 / width)
        )
        low_ref[own, :] = (inv_ref[own, :1] * (total_ref[own, :] - inner)).astype(BF16)
    saves[2].start()
    up = dot(turned_ref[:HALO, :HALO], low_ref[:HALO, :]) * (1.0 / NEIGH)
    rim_ref[1 - core] = up.astype(BF16)
    down = dot(turned_ref[cells + HALO :, cells - HALO :], low_ref[cells - HALO :, :]) * (1.0 / NEIGH)
    rim_ref[core] = down.astype(BF16)
    saves[0].start()
    saves[1].start()
    for save in saves:
        save.wait()


def pair_kernel(fields, keep_ref, got_ref, out_ref):
    last = keep_ref.shape[1] - 1
    for k in range(keep_ref.shape[0]):
        total = keep_ref[k, :last].astype(F32) + got_ref[k, :last].astype(F32)
        out_ref[k, :last] = total.astype(BF16)
        tile = keep_ref[k, last].astype(F32) + got_ref[k, last].astype(F32)
        out_ref[k, last] = split_loss(tile, read_loss(tile, fields), fields).astype(BF16)


def plane_kernel(fields, parts_ref, out_ref):
    me = lax.axis_index("xh") * lax.axis_size("y") + lax.axis_index("y")
    blocks = parts_ref.shape[1] - 1
    for j in range(blocks + 1):
        total = parts_ref[0, j].astype(F32)
        for k in range(1, parts_ref.shape[0]):
            total = total + parts_ref[k, j].astype(F32)
        if j < blocks:
            out_ref[j, 0] = total.astype(BF16)
    loss = read_loss(total, fields)
    for j in range(blocks):
        tile = jnp.where(me == j, total, 0.0)
        out_ref[j, 1] = split_loss(tile, loss, fields).astype(BF16)


def fold_kernel(fields, parts_ref, out_ref):
    total = parts_ref[0].astype(F32)
    for k in range(1, parts_ref.shape[0]):
        total = total + parts_ref[k].astype(F32)
    first = total[0].astype(BF16)
    second = split_loss(total[1], read_loss(total[1], fields), fields).astype(BF16)
    for m in range(out_ref.shape[0]):
        out_ref[m, 0] = first
        out_ref[m, 1] = second


def last_kernel(fields, patches, parts_ref, first_ref, second_ref, loss_ref):
    members = parts_ref.shape[0]
    for m in range(members):
        first_ref[:, m * LANES : (m + 1) * LANES] = parts_ref[member_place(m, members), 0].astype(F32)
    tile = parts_ref[member_place(lax.axis_index("z"), members), 1].astype(F32)
    second_ref[...] = tile[:, :fields]
    loss_ref[...] = read_loss(tile, fields)[:1, :] * (1.0 / patches)


def gather_kernel(low_hbm, turned_hbm, same_ref, other_ref, grad_ref, low_ref, turned_ref, done):
    loads = [
        pltpu.make_async_copy(low_hbm, low_ref, done.at[0]),
        pltpu.make_async_copy(turned_hbm, turned_ref, done.at[1]),
    ]
    for load in loads:
        load.start()
    for load in loads:
        load.wait()
    core = lax.axis_index("co")
    blocks = low_ref.shape[0] // HALO
    for row in range(1, blocks + 1):
        near = slice(max(row - 2, 0) * HALO, min(row + 1, blocks) * HALO)
        back = dot(turned_ref[row * HALO : (row + 1) * HALO, near], low_ref[near, :]) * (1.0 / NEIGH)
        if row == 1:
            back = back + jnp.where(core == 0, other_ref[...], same_ref[...]).astype(F32)
        if row == blocks:
            back = back + jnp.where(core == 0, same_ref[...], other_ref[...]).astype(F32)
        grad_ref[(row - 1) * HALO : row * HALO, :] = back.astype(BF16)


BAND = ("z", "xl", "co")
MEM = ("xh", "y")
PLANE = ("y", "xh", "xl")


def member_groups(bands, members):
    groups = []
    for band in range(bands):
        group = [band * members + m for m in range(members)]
        groups.append(group if band % 2 == 0 else group[::-1])
    return groups


def member_place(member, members):
    return jnp.where(lax.axis_index("co") == 0, member, members - 1 - member)


def per_device(hidden, gain, w_first, w_second, target, patch_ids, neighbours):
    states = hidden[0]
    cells, width = states.shape
    fields = w_second.shape[1]
    bands, members = lax.axis_size(BAND), lax.axis_size(MEM)
    share = width // bands
    chips = [(i, i + 1) for i in range(1, bands - 1, 2)]
    chips = chips + [(j, i) for i, j in chips]
    cores = [(0, 1), (1, 0)]
    rim_same, rim_other = call(
        rims_kernel,
        [shape((HALO, width), BF16), shape((HALO, width), BF16)],
        [states],
        0,
        4,
        [pltpu.SemaphoreType.DMA((2,))],
        anywhere=(0,),
        held=(0, 1),
    )
    same = lax.ppermute(rim_same, "co", cores)
    other = lax.ppermute(rim_other, BAND, chips)
    held = cells - HALO
    saved = [shape((held, width), BF16)] * 3 + [shape((held, LANES), F32)]
    *inside, gain, first, second, partial, outside, turned, first_turned, turned_saved = call(
        inner_kernel,
        [
            shape((fields, held), BF16),
            *saved,
            shape((1, width), F32),
            shape(w_first.shape, BF16),
            shape((fields, width), BF16),
            shape((HALO, width), F32),
            shape((HALO, HALO), BF16),
            shape((cells + 2 * HALO, cells), BF16),
            shape(w_first.shape[::-1], BF16),
            shape((cells + 2 * HALO, cells), BF16),
        ],
        [same, neighbours, states, gain[None], w_first, w_second.T],
        10**9,
        16,
        [
            pltpu.VMEM(neighbours.shape, jnp.int32),
            pltpu.VMEM(states.shape, BF16),
            pltpu.SemaphoreType.DMA((6,)),
        ],
        anywhere=(1, 2, 3, 4, 5),
        stored=(12,),
        held=(5, 6, 7, 10, 11),
    )
    saved = [shape((cells, width), BF16)] * 3 + [shape((cells, LANES), F32)]
    copies, slope, active, normed, inv_root = call(
        outer_kernel,
        [shape((members, fields, cells), BF16)] + saved,
        [other, partial, outside, gain, second, *inside, first],
        10**9,
        20,
        [pltpu.VMEM((HALO, width), BF16)],
    )
    groups = member_groups(bands, members)
    everyone = lax.all_to_all(copies, BAND + MEM, 0, 0, axis_index_groups=groups)
    message = (2 * members, members + 1, share, LANES)
    keep, send, d_pre = call(
        score_kernel,
        [shape(message, BF16), shape(message, BF16), shape((cells, width), BF16)],
        [everyone, target, patch_ids[None], second, slope, active, normed],
        2 * 10**9,
        20,
    )
    got = lax.ppermute(send, "co", cores)
    low, rim_same, rim_other = call(
        backward_kernel,
        [
            shape((cells, width), BF16),
            shape((HALO, width), BF16),
            shape((HALO, width), BF16),
        ],
        [first_turned, d_pre, normed, inv_root, turned, gain],
        2 * 10**9,
        20,
        [
            pltpu.VMEM((cells, width), F32),
            pltpu.VMEM((cells, width), BF16),
            pltpu.VMEM((2, HALO, width), BF16),
            pltpu.SemaphoreType.DMA((3,)),
        ],
        stored=(0, 1, 2),
    )
    got, low = lax.optimization_barrier((got, low))
    (mine,) = call(
        functools.partial(pair_kernel, fields), [shape(message, BF16)], [keep, got], 10**6, 8
    )
    parts = lax.all_to_all(mine, PLANE, 0, 0)
    parts, rim_same, rim_other = lax.optimization_barrier((parts, rim_same, rim_other))
    same = lax.ppermute(rim_same, "co", cores)
    other = lax.ppermute(rim_other, BAND, chips)
    (grad_hidden,) = call(
        gather_kernel,
        [shape((cells, width), BF16)],
        [low, turned_saved, same, other],
        0,
        16,
        [
            pltpu.VMEM((cells, width), BF16),
            pltpu.VMEM(turned.shape, BF16),
            pltpu.SemaphoreType.DMA((2,)),
        ],
        anywhere=(0, 1),
    )
    message = (members, 2, share, LANES)
    (planed,) = call(
        functools.partial(plane_kernel, fields), [shape(message, BF16)], [parts], 10**6, 8
    )
    parts = lax.all_to_all(planed, "z", 0, 0)
    (folded,) = call(
        functools.partial(fold_kernel, fields), [shape(message, BF16)], [parts], 10**6, 8
    )
    parts = lax.all_to_all(folded, BAND + MEM, 0, 0, axis_index_groups=groups)
    grad_first, grad_second, loss = call(
        functools.partial(last_kernel, fields, cells // PATCH * bands),
        [shape((share, width), F32), shape((share, fields), F32), shape((1, 1), F32)],
        [parts],
        10**6,
        8,
    )
    return (loss[0, 0], grad_hidden[None], grad_first, grad_second)


def solution(mesh):
    split = jax.sharding.Mesh(mesh.devices.reshape(8, 2, 2, 2, 4), BAND + MEM)
    return jax.shard_map(
        per_device,
        mesh=split,
        in_specs=(
            P(MEM, BAND, None),
            P(),
            P(),
            P(),
            P(None, BAND),
            P(BAND),
            P(None, BAND),
        ),
        out_specs=(P(), P(MEM, BAND, None), P(BAND, None), P(BAND, None)),
        check_vma=False,
    )
```

```python
import functools
import math

import jax
import jax.numpy as jnp
from jax import lax
from jax.experimental import pallas as pl
from jax.experimental.pallas import tpu as pltpu
from jax.sharding import PartitionSpec as P

PATCH = 256
NEIGH = 6
HALO = 128
EPS_NORM = 1e-05
EPS_DIST = 1e-06
LANES = 128
F32 = jnp.float32
BF16 = jnp.bfloat16
VMEM = pl.BlockSpec(memory_space=pltpu.VMEM)
ANY = pl.BlockSpec(memory_space=pl.ANY)


def dot(a, b, ca=1, cb=0):
    return lax.dot_general(a, b, (((ca,), (cb,)), ((), ())), preferred_element_type=F32)


def call(kernel, outs, args, flops, limit, scratch=(), anywhere=(), stored=(), held=()):
    args = [
        pltpu.with_memory_space_constraint(a, pltpu.HBM) if i in anywhere else a
        for i, a in enumerate(args)
    ]
    moved = sum(math.prod(a.shape) * a.dtype.itemsize for a in list(args) + list(outs))
    return pl.pallas_call(
        kernel,
        out_shape=[
            pltpu.HBM(o.shape, o.dtype) if i in stored else pltpu.VMEM(o.shape, o.dtype) if i in held else o
            for i, o in enumerate(outs)
        ],
        in_specs=[ANY if i in anywhere else VMEM for i in range(len(args))],
        out_specs=[ANY if i in stored else VMEM for i in range(len(outs))],
        scratch_shapes=list(scratch),
        compiler_params=pltpu.CompilerParams(vmem_limit_bytes=limit * 2**20),
        cost_estimate=pl.CostEstimate(flops=flops, bytes_accessed=moved, transcendentals=0)
        if flops
        else None,
    )(*args)


def shape(dims, kind):
    return jax.ShapeDtypeStruct(dims, kind)


def rims_kernel(states_hbm, same_ref, other_ref, done):
    rows = states_hbm.shape[0]
    core = lax.axis_index("co")
    low, high = core * (rows - HALO), (1 - core) * (rows - HALO)
    moves = [
        pltpu.make_async_copy(states_hbm.at[pl.ds(low, HALO)], other_ref, done.at[0]),
        pltpu.make_async_copy(states_hbm.at[pl.ds(high, HALO)], same_ref, done.at[1]),
    ]
    for move in moves:
        move.start()
    for move in moves:
        move.wait()


def count_rows(near, block):
    near = near[:, block * HALO : (block + 1) * HALO]
    row = lax.broadcasted_iota(jnp.int32, (3 * HALO, HALO), 0)
    own = lax.broadcasted_iota(jnp.int32, (3 * HALO, HALO), 1) + HALO
    total = jnp.where(row == own, float(NEIGH), 0.0)
    for k in range(NEIGH):
        total = total + jnp.where(near[k : k + 1, :] == row + block * HALO, 1.0, 0.0)
    return total


def normalise(summed, gain):
    centred = summed - jnp.mean(summed, -1, keepdims=True)
    inv_root = lax.rsqrt(jnp.mean(centred * centred, -1, keepdims=True) + EPS_NORM)
    normed = (centred * inv_root * gain).astype(BF16)
    return normed, jnp.broadcast_to(inv_root, (summed.shape[0], LANES))


def head(normed_ref, first_ref, part):
    preact = dot(normed_ref[...], first_ref[:, part])
    share = 0.5 * (1.0 + lax.erf(preact * math.sqrt(0.5)))
    bell = jnp.exp(-0.5 * preact * preact) * (1.0 / math.sqrt(2.0 * math.pi))
    return (preact * share).astype(BF16), (share + preact * bell).astype(BF16)


def inner_kernel(
    same_ref, near_hbm, states_hbm, gain_hbm, first_hbm, second_hbm,
    predicted_ref, slope_ref, active_ref, normed_ref, inv_ref, gain_ref, first_ref, second_ref,
    partial_ref, outside_ref, turned_ref, first_turned_ref, turned_hbm,
    near_ref, states_ref, done,
):
    loads = [
        pltpu.make_async_copy(source, place, done.at[i])
        for i, (source, place) in enumerate(
            [
                (near_hbm, near_ref),
                (states_hbm, states_ref),
                (gain_hbm, gain_ref),
                (first_hbm, first_ref),
                (second_hbm, second_ref),
            ]
        )
    ]
    for load in loads:
        load.start()
    core = lax.axis_index("co")
    loads[0].wait()
    near = near_ref[...]
    cells = states_ref.shape[0]
    blocks = cells // HALO
    counts = []
    for block in range(blocks):
        total = count_rows(near, block)
        turned_ref[block * HALO : (block + 3) * HALO, block * HALO : (block + 1) * HALO] = total.astype(BF16)
        counts.append(total.T.astype(BF16))
    save = pltpu.make_async_copy(turned_ref, turned_hbm, done.at[5])
    save.start()
    outside = (counts[0][:, :HALO], counts[-1][:, 2 * HALO :])
    inside = (counts[0][:, HALO:], counts[-1][:, : 2 * HALO])
    loads[1].wait()
    loads[2].wait()
    gain = gain_ref[...]
    for block in range(1, blocks - 1):
        reach = states_ref[(block - 1) * HALO : (block + 2) * HALO, :]
        summed = dot(counts[block], reach) * (1.0 / NEIGH)
        to = slice((block - 1) * HALO, block * HALO)
        normed_ref[to, :], inv_ref[to, :] = normalise(summed, gain)
    last = cells - 2 * HALO
    rows = states_ref[pl.ds(pl.multiple_of((1 - core) * last, HALO), 2 * HALO), :]
    summed = dot(jnp.where(core == 0, inside[1], inside[0]), rows)
    summed = summed + dot(jnp.where(core == 0, outside[1], outside[0]), same_ref[...])
    normed_ref[last:, :], inv_ref[last:, :] = normalise(summed * (1.0 / NEIGH), gain)
    rows = states_ref[pl.ds(pl.multiple_of(core * last, HALO), 2 * HALO), :]
    partial_ref[...] = dot(jnp.where(core == 0, inside[0], inside[1]), rows)
    outside_ref[...] = jnp.where(core == 0, outside[0], outside[1])
    loads[3].wait()
    loads[4].wait()
    cols = 256
    for n in range(0, normed_ref.shape[1], cols):
        part = slice(n, n + cols)
        active_ref[:, part], slope_ref[:, part] = head(normed_ref, first_ref, part)
    predicted_ref[...] = dot(second_ref[...], active_ref[...], 1, 1).astype(BF16)
    for n in range(0, first_ref.shape[0], LANES):
        first_turned_ref[:, n : n + LANES] = first_ref[n : n + LANES, :].T
    save.wait()


def outer_kernel(
    other_ref, partial_ref, outside_ref, gain_ref, second_ref,
    predicted_in_ref, slope_in_ref, active_in_ref, normed_in_ref, inv_in_ref, first_ref,
    copies_ref, slope_ref, active_ref, normed_ref, inv_ref,
    own_ref,
):
    cells, width = normed_ref.shape
    core = lax.axis_index("co")
    last = cells - HALO
    inner, held = slice(HALO, last), slice(0, last - HALO)
    mine = pl.ds(pl.multiple_of(core * last, HALO), HALO)
    done = pl.ds(pl.multiple_of((1 - core) * last, HALO), HALO)
    summed = (partial_ref[...] + dot(outside_ref[...], other_ref[...])) * (1.0 / NEIGH)
    normed, inv_ref[mine, :] = normalise(summed, gain_ref[...])
    normed_ref[mine, :] = normed
    own_ref[...] = normed
    for full_ref, part_ref in (
        (normed_ref, normed_in_ref),
        (inv_ref, inv_in_ref),
        (active_ref, active_in_ref),
        (slope_ref, slope_in_ref),
    ):
        full_ref[inner, :] = part_ref[held, :]
        full_ref[done, :] = part_ref[last - HALO :, :]
    cols = 256
    for n in range(0, width, cols):
        part = slice(n, n + cols)
        active_ref[mine, part], slope_ref[mine, part] = head(own_ref, first_ref, part)
    predicted = dot(second_ref[...], active_ref[mine, :], 1, 1).astype(BF16)
    for m in range(copies_ref.shape[0]):
        copies_ref[m, :, inner] = predicted_in_ref[:, held]
        copies_ref[m, :, done] = predicted_in_ref[:, last - HALO :]
        copies_ref[m, :, mine] = predicted


def split_loss(tile, loss, fields):
    lane = lax.broadcasted_iota(jnp.int32, tile.shape, 1)
    high = loss.astype(BF16).astype(F32)
    low = loss - high
    return jnp.where(lane == fields, high, jnp.where(lane == fields + 1, low, tile))


def read_loss(tile, fields):
    lane = lax.broadcasted_iota(jnp.int32, tile.shape, 1)
    here = (lane == fields) | (lane == fields + 1)
    return jnp.sum(jnp.where(here, tile, 0.0), axis=1, keepdims=True)


def score_kernel(
    everyone_ref, target_ref, patch_ref, second_ref, slope_ref, active_ref, normed_ref,
    keep_ref, send_ref, dpre_ref,
):
    members, fields, cells = everyone_ref.shape
    width = slope_ref.shape[1]
    me = member_place(lax.axis_index("xh") * lax.axis_size("y") + lax.axis_index("y"), members)
    entries = fields * PATCH
    share = keep_ref.shape[2]

    def target_of(xl, member):
        return (member % 4) * 4 + (member // 4) * 2 + xl

    places = [(b, ((b // 2) % 2, b // 4)) for b in range(width // share)]
    own = everyone_ref[me].astype(F32)
    error = own - target_ref[...]
    sums = [jnp.sum(error * error, axis=0, keepdims=True)]
    for n in range(members):
        differ = own - everyone_ref[n].astype(F32)
        sums.append(jnp.sum(differ * differ, axis=0, keepdims=True))
    sums.append(jnp.zeros((16 - len(sums), cells), F32))
    sums = jnp.concatenate(sums, 0)
    even = (patch_ref[...] & 1) == 0
    spread_even = jnp.sqrt(jnp.sum(jnp.where(even, sums, 0.0), 1, keepdims=True) / entries + EPS_DIST)
    spread_odd = jnp.sqrt(jnp.sum(jnp.where(even, 0.0, sums), 1, keepdims=True) / entries + EPS_DIST)
    row = lax.broadcasted_iota(jnp.int32, (16, 1), 0)
    weight = jnp.where(row == 0, 1.0 / members, 1.0 / (members * (members - 1)))
    scale = jnp.where(even, weight / spread_even, weight / spread_odd)
    gradient = error * scale[0:1]
    for n in range(members):
        differ = own - everyone_ref[n].astype(F32)
        gradient = gradient - differ * scale[n + 1 : n + 2]
    both = spread_even + spread_odd
    used = jnp.where(row == 0, 1.0 / members, -0.5 / (members * (members - 1)))
    used = jnp.where((row == me + 1) | (row > members), 0.0, used)
    loss = jnp.sum(both * used, axis=0, keepdims=True)

    gradient = jnp.concatenate([gradient, jnp.zeros((LANES - fields, cells), F32)], 0)
    outer = gradient.T.astype(BF16)
    cols = 256
    for n in range(0, width, cols):
        part = slice(n, n + cols)
        d_active = dot(outer[:, :fields], second_ref[:, part])
        dpre_ref[:, part] = (d_active * slope_ref[:, part].astype(F32)).astype(BF16)

    def weight_grads(kept):
        for n in range(0, width, cols):
            grad = dot(normed_ref[...], dpre_ref[:, n : n + cols], 0, 0).astype(BF16)
            for band, slot in places:
                to_ref = keep_ref if band % 2 == kept else send_ref
                rows = grad[band * share : (band + 1) * share]
                for c in range(0, cols, LANES):
                    to_ref[target_of(slot[0], (n + c) // LANES), slot[1]] = rows[:, c : c + LANES]
        grad = dot(active_ref[...], outer, 0, 0)
        grad = split_loss(grad, loss, fields).astype(BF16)
        for band, slot in places:
            to_ref = keep_ref if band % 2 == kept else send_ref
            to_ref[target_of(slot[0], slot[1]), members] = grad[band * share : (band + 1) * share]

    core = lax.axis_index("co")
    pl.when(core == 0)(lambda: weight_grads(0))
    pl.when(core == 1)(lambda: weight_grads(1))


def backward_kernel(
    first_ref, dpre_ref, normed_ref, inv_ref, turned_ref, gain_ref,
    low_hbm, same_hbm, other_hbm,
    total_ref, low_ref, rim_ref, done,
):
    cells, width = low_ref.shape
    blocks = cells // HALO
    gain = gain_ref[...]
    inverse = 1.0 / gain
    core = lax.axis_index("co")
    saves = [
        pltpu.make_async_copy(source, place, done.at[i])
        for i, (source, place) in enumerate(
            [
                (rim_ref.at[0], same_hbm),
                (rim_ref.at[1], other_hbm),
                (low_ref, low_hbm),
            ]
        )
    ]
    cols = 256
    mean = jnp.zeros((cells, LANES), F32)
    along = jnp.zeros((cells, LANES), F32)
    for n in range(0, width, cols):
        part = slice(n, n + cols)
        d_normed = dot(dpre_ref[...], first_ref[:, part])
        scaled = d_normed * gain[:, part]
        total_ref[:, part] = scaled
        shared = d_normed * normed_ref[:, part].astype(F32)
        for c in range(0, cols, LANES):
            mean = mean + scaled[:, c : c + LANES]
            along = along + shared[:, c : c + LANES]
    mean = jnp.sum(mean, -1, keepdims=True)
    along = jnp.sum(along, -1, keepdims=True)
    for block in (0, blocks - 1, *range(1, blocks - 1)):
        own = slice(block * HALO, (block + 1) * HALO)
        inner = mean[own] * (1.0 / width) + normed_ref[own, :].astype(F32) * inverse * (
            along[own] * (1.0 / width)
        )
        low_ref[own, :] = (inv_ref[own, :1] * (total_ref[own, :] - inner)).astype(BF16)
    saves[2].start()
    up = dot(turned_ref[:HALO, :HALO], low_ref[:HALO, :]) * (1.0 / NEIGH)
    rim_ref[1 - core] = up.astype(BF16)
    down = dot(turned_ref[cells + HALO :, cells - HALO :], low_ref[cells - HALO :, :]) * (1.0 / NEIGH)
    rim_ref[core] = down.astype(BF16)
    saves[0].start()
    saves[1].start()
    for save in saves:
        save.wait()


def pair_kernel(fields, keep_ref, got_ref, out_ref):
    last = keep_ref.shape[1] - 1
    for k in range(keep_ref.shape[0]):
        total = keep_ref[k, :last].astype(F32) + got_ref[k, :last].astype(F32)
        out_ref[k, :last] = total.astype(BF16)
        tile = keep_ref[k, last].astype(F32) + got_ref[k, last].astype(F32)
        out_ref[k, last] = split_loss(tile, read_loss(tile, fields), fields).astype(BF16)


def plane_kernel(fields, parts_ref, out_ref):
    me = lax.axis_index("xh") * lax.axis_size("y") + lax.axis_index("y")
    blocks = parts_ref.shape[1] - 1
    for j in range(blocks + 1):
        total = parts_ref[0, j].astype(F32)
        for k in range(1, parts_ref.shape[0]):
            total = total + parts_ref[k, j].astype(F32)
        if j < blocks:
            out_ref[member_place(j, blocks), 0] = total.astype(BF16)
    loss = read_loss(total, fields)
    for j in range(blocks):
        tile = jnp.where(me == j, total, 0.0)
        out_ref[member_place(j, blocks), 1] = split_loss(tile, loss, fields).astype(BF16)


def fold_kernel(fields, parts_ref, out_ref):
    total = parts_ref[0].astype(F32)
    for k in range(1, parts_ref.shape[0]):
        total = total + parts_ref[k].astype(F32)
    first = total[0].astype(BF16)
    second = split_loss(total[1], read_loss(total[1], fields), fields).astype(BF16)
    for m in range(out_ref.shape[0]):
        out_ref[m, 0] = first
        out_ref[m, 1] = second


def last_kernel(fields, patches, parts_ref, first_ref, second_ref, loss_ref):
    members = parts_ref.shape[0]
    for m in range(members):
        first_ref[:, m * LANES : (m + 1) * LANES] = parts_ref[member_place(m, members), 0].astype(F32)
    tile = parts_ref[member_place(lax.axis_index("z"), members), 1].astype(F32)
    second_ref[...] = tile[:, :fields]
    loss_ref[...] = read_loss(tile, fields)[:1, :] * (1.0 / patches)


def gather_kernel(low_hbm, turned_hbm, same_ref, other_ref, grad_ref, low_ref, turned_ref, done):
    loads = [
        pltpu.make_async_copy(low_hbm, low_ref, done.at[0]),
        pltpu.make_async_copy(turned_hbm, turned_ref, done.at[1]),
    ]
    for load in loads:
        load.start()
    for load in loads:
        load.wait()
    core = lax.axis_index("co")
    blocks = low_ref.shape[0] // HALO
    for row in range(1, blocks + 1):
        near = slice(max(row - 2, 0) * HALO, min(row + 1, blocks) * HALO)
        back = dot(turned_ref[row * HALO : (row + 1) * HALO, near], low_ref[near, :]) * (1.0 / NEIGH)
        if row == 1:
            back = back + jnp.where(core == 0, other_ref[...], same_ref[...]).astype(F32)
        if row == blocks:
            back = back + jnp.where(core == 0, same_ref[...], other_ref[...]).astype(F32)
        grad_ref[(row - 1) * HALO : row * HALO, :] = back.astype(BF16)


BAND = ("z", "xl", "co")
MEM = ("xh", "y")
PLANE = ("y", "xh", "xl")


def member_groups(bands, members):
    groups = []
    for band in range(bands):
        group = [band * members + m for m in range(members)]
        groups.append(group if band % 2 == 0 else group[::-1])
    return groups


def height_groups(bands, members):
    groups = []
    for i in range(4 * members):
        group = [(z * 4 + i // members) * members + i % members for z in range(bands // 4)]
        groups.append(group if i // members % 2 == 0 else group[::-1])
    return groups


def member_place(member, members):
    return jnp.where(lax.axis_index("co") == 0, member, members - 1 - member)


def per_device(hidden, gain, w_first, w_second, target, patch_ids, neighbours):
    states = hidden[0]
    cells, width = states.shape
    fields = w_second.shape[1]
    bands, members = lax.axis_size(BAND), lax.axis_size(MEM)
    share = width // bands
    chips = [(i, i + 1) for i in range(1, bands - 1, 2)]
    chips = chips + [(j, i) for i, j in chips]
    cores = [(0, 1), (1, 0)]
    rim_same, rim_other = call(
        rims_kernel,
        [shape((HALO, width), BF16), shape((HALO, width), BF16)],
        [states],
        0,
        4,
        [pltpu.SemaphoreType.DMA((2,))],
        anywhere=(0,),
        held=(0, 1),
    )
    same = lax.ppermute(rim_same, "co", cores)
    other = lax.ppermute(rim_other, BAND, chips)
    held = cells - HALO
    saved = [shape((held, width), BF16)] * 3 + [shape((held, LANES), F32)]
    *inside, gain, first, second, partial, outside, turned, first_turned, turned_saved = call(
        inner_kernel,
        [
            shape((fields, held), BF16),
            *saved,
            shape((1, width), F32),
            shape(w_first.shape, BF16),
            shape((fields, width), BF16),
            shape((HALO, width), F32),
            shape((HALO, HALO), BF16),
            shape((cells + 2 * HALO, cells), BF16),
            shape(w_first.shape[::-1], BF16),
            shape((cells + 2 * HALO, cells), BF16),
        ],
        [same, neighbours, states, gain[None], w_first, w_second.T],
        10**9,
        16,
        [
            pltpu.VMEM(neighbours.shape, jnp.int32),
            pltpu.VMEM(states.shape, BF16),
            pltpu.SemaphoreType.DMA((6,)),
        ],
        anywhere=(1, 2, 3, 4, 5),
        stored=(12,),
        held=(5, 6, 7, 10, 11),
    )
    saved = [shape((cells, width), BF16)] * 3 + [shape((cells, LANES), F32)]
    copies, slope, active, normed, inv_root = call(
        outer_kernel,
        [shape((members, fields, cells), BF16)] + saved,
        [other, partial, outside, gain, second, *inside, first],
        10**9,
        20,
        [pltpu.VMEM((HALO, width), BF16)],
    )
    groups = member_groups(bands, members)
    everyone = lax.all_to_all(copies, BAND + MEM, 0, 0, axis_index_groups=groups)
    message = (2 * members, members + 1, share, LANES)
    keep, send, d_pre = call(
        score_kernel,
        [shape(message, BF16), shape(message, BF16), shape((cells, width), BF16)],
        [everyone, target, patch_ids[None], second, slope, active, normed],
        2 * 10**9,
        20,
    )
    got = lax.ppermute(send, "co", cores)
    low, rim_same, rim_other = call(
        backward_kernel,
        [
            shape((cells, width), BF16),
            shape((HALO, width), BF16),
            shape((HALO, width), BF16),
        ],
        [first_turned, d_pre, normed, inv_root, turned, gain],
        2 * 10**9,
        20,
        [
            pltpu.VMEM((cells, width), F32),
            pltpu.VMEM((cells, width), BF16),
            pltpu.VMEM((2, HALO, width), BF16),
            pltpu.SemaphoreType.DMA((3,)),
        ],
        stored=(0, 1, 2),
    )
    got, low = lax.optimization_barrier((got, low))
    (mine,) = call(
        functools.partial(pair_kernel, fields), [shape(message, BF16)], [keep, got], 10**6, 8
    )
    parts = lax.all_to_all(mine, PLANE, 0, 0)
    parts, rim_same, rim_other = lax.optimization_barrier((parts, rim_same, rim_other))
    same = lax.ppermute(rim_same, "co", cores)
    other = lax.ppermute(rim_other, BAND, chips)
    (grad_hidden,) = call(
        gather_kernel,
        [shape((cells, width), BF16)],
        [low, turned_saved, same, other],
        0,
        16,
        [
            pltpu.VMEM((cells, width), BF16),
            pltpu.VMEM(turned.shape, BF16),
            pltpu.SemaphoreType.DMA((2,)),
        ],
        anywhere=(0, 1),
    )
    message = (members, 2, share, LANES)
    (planed,) = call(
        functools.partial(plane_kernel, fields), [shape(message, BF16)], [parts], 10**6, 8
    )
    heights = height_groups(bands, members)
    parts = lax.all_to_all(planed, BAND + MEM, 0, 0, axis_index_groups=heights)
    (folded,) = call(
        functools.partial(fold_kernel, fields), [shape(message, BF16)], [parts], 10**6, 8
    )
    parts = lax.all_to_all(folded, BAND + MEM, 0, 0, axis_index_groups=groups)
    grad_first, grad_second, loss = call(
        functools.partial(last_kernel, fields, cells // PATCH * bands),
        [shape((share, width), F32), shape((share, fields), F32), shape((1, 1), F32)],
        [parts],
        10**6,
        8,
    )
    return (loss[0, 0], grad_hidden[None], grad_first, grad_second)


def solution(mesh):
    split = jax.sharding.Mesh(mesh.devices.reshape(8, 2, 2, 2, 4), BAND + MEM)
    return jax.shard_map(
        per_device,
        mesh=split,
        in_specs=(
            P(MEM, BAND, None),
            P(),
            P(),
            P(),
            P(None, BAND),
            P(BAND),
            P(None, BAND),
        ),
        out_specs=(P(), P(MEM, BAND, None), P(BAND, None), P(BAND, None)),
        check_vma=False,
    )
```

```python
import functools
import math

import jax
import jax.numpy as jnp
from jax import lax
from jax.experimental import pallas as pl
from jax.experimental.pallas import tpu as pltpu
from jax.sharding import PartitionSpec as P

PATCH = 256
NEIGH = 6
HALO = 128
EPS_NORM = 1e-05
EPS_DIST = 1e-06
LANES = 128
F32 = jnp.float32
BF16 = jnp.bfloat16
VMEM = pl.BlockSpec(memory_space=pltpu.VMEM)
ANY = pl.BlockSpec(memory_space=pl.ANY)


def dot(a, b, ca=1, cb=0):
    return lax.dot_general(a, b, (((ca,), (cb,)), ((), ())), preferred_element_type=F32)


def call(kernel, outs, args, flops, limit, scratch=(), anywhere=(), stored=(), held=()):
    args = [
        pltpu.with_memory_space_constraint(a, pltpu.HBM) if i in anywhere else a
        for i, a in enumerate(args)
    ]
    moved = sum(math.prod(a.shape) * a.dtype.itemsize for a in list(args) + list(outs))
    return pl.pallas_call(
        kernel,
        out_shape=[
            pltpu.HBM(o.shape, o.dtype) if i in stored else pltpu.VMEM(o.shape, o.dtype) if i in held else o
            for i, o in enumerate(outs)
        ],
        in_specs=[ANY if i in anywhere else VMEM for i in range(len(args))],
        out_specs=[ANY if i in stored else VMEM for i in range(len(outs))],
        scratch_shapes=list(scratch),
        compiler_params=pltpu.CompilerParams(vmem_limit_bytes=limit * 2**20),
        cost_estimate=pl.CostEstimate(flops=flops, bytes_accessed=moved, transcendentals=0)
        if flops
        else None,
    )(*args)


def shape(dims, kind):
    return jax.ShapeDtypeStruct(dims, kind)


def rims_kernel(states_hbm, same_ref, other_ref, done):
    rows = states_hbm.shape[0]
    core = lax.axis_index("co")
    low, high = core * (rows - HALO), (1 - core) * (rows - HALO)
    moves = [
        pltpu.make_async_copy(states_hbm.at[pl.ds(low, HALO)], other_ref, done.at[0]),
        pltpu.make_async_copy(states_hbm.at[pl.ds(high, HALO)], same_ref, done.at[1]),
    ]
    for move in moves:
        move.start()
    for move in moves:
        move.wait()


def count_rows(near, block):
    near = near[:, block * HALO : (block + 1) * HALO]
    row = lax.broadcasted_iota(jnp.int32, (3 * HALO, HALO), 0)
    own = lax.broadcasted_iota(jnp.int32, (3 * HALO, HALO), 1) + HALO
    total = jnp.where(row == own, float(NEIGH), 0.0)
    for k in range(NEIGH):
        total = total + jnp.where(near[k : k + 1, :] == row + block * HALO, 1.0, 0.0)
    return total


def normalise(summed, gain):
    centred = summed - jnp.mean(summed, -1, keepdims=True)
    inv_root = lax.rsqrt(jnp.mean(centred * centred, -1, keepdims=True) + EPS_NORM)
    normed = (centred * inv_root * gain).astype(BF16)
    return normed, jnp.broadcast_to(inv_root, (summed.shape[0], LANES))


def head(normed_ref, first_ref, part):
    preact = dot(normed_ref[...], first_ref[:, part])
    share = 0.5 * (1.0 + lax.erf(preact * math.sqrt(0.5)))
    bell = jnp.exp(-0.5 * preact * preact) * (1.0 / math.sqrt(2.0 * math.pi))
    return (preact * share).astype(BF16), (share + preact * bell).astype(BF16)


def inner_kernel(
    same_ref, near_hbm, states_hbm, gain_hbm, first_hbm, second_hbm,
    predicted_ref, slope_ref, active_ref, normed_ref, inv_ref, gain_ref, first_ref, second_ref,
    partial_ref, outside_ref, turned_ref, first_turned_ref, turned_hbm,
    near_ref, states_ref, done,
):
    loads = [
        pltpu.make_async_copy(source, place, done.at[i])
        for i, (source, place) in enumerate(
            [
                (near_hbm, near_ref),
                (states_hbm, states_ref),
                (gain_hbm, gain_ref),
                (first_hbm, first_ref),
                (second_hbm, second_ref),
            ]
        )
    ]
    for load in loads:
        load.start()
    core = lax.axis_index("co")
    loads[0].wait()
    near = near_ref[...]
    cells = states_ref.shape[0]
    blocks = cells // HALO
    counts = []
    for block in range(blocks):
        total = count_rows(near, block)
        turned_ref[block * HALO : (block + 3) * HALO, block * HALO : (block + 1) * HALO] = total.astype(BF16)
        counts.append(total.T.astype(BF16))
    save = pltpu.make_async_copy(turned_ref, turned_hbm, done.at[5])
    save.start()
    outside = (counts[0][:, :HALO], counts[-1][:, 2 * HALO :])
    inside = (counts[0][:, HALO:], counts[-1][:, : 2 * HALO])
    loads[1].wait()
    loads[2].wait()
    gain = gain_ref[...]
    for block in range(1, blocks - 1):
        reach = states_ref[(block - 1) * HALO : (block + 2) * HALO, :]
        summed = dot(counts[block], reach) * (1.0 / NEIGH)
        to = slice((block - 1) * HALO, block * HALO)
        normed_ref[to, :], inv_ref[to, :] = normalise(summed, gain)
    last = cells - 2 * HALO
    rows = states_ref[pl.ds(pl.multiple_of((1 - core) * last, HALO), 2 * HALO), :]
    summed = dot(jnp.where(core == 0, inside[1], inside[0]), rows)
    summed = summed + dot(jnp.where(core == 0, outside[1], outside[0]), same_ref[...])
    normed_ref[last:, :], inv_ref[last:, :] = normalise(summed * (1.0 / NEIGH), gain)
    rows = states_ref[pl.ds(pl.multiple_of(core * last, HALO), 2 * HALO), :]
    partial_ref[...] = dot(jnp.where(core == 0, inside[0], inside[1]), rows)
    outside_ref[...] = jnp.where(core == 0, outside[0], outside[1])
    loads[3].wait()
    loads[4].wait()
    cols = 256
    for n in range(0, normed_ref.shape[1], cols):
        part = slice(n, n + cols)
        active_ref[:, part], slope_ref[:, part] = head(normed_ref, first_ref, part)
    predicted_ref[...] = dot(second_ref[...], active_ref[...], 1, 1).astype(BF16)
    for n in range(0, first_ref.shape[0], LANES):
        first_turned_ref[:, n : n + LANES] = first_ref[n : n + LANES, :].T
    save.wait()


def outer_kernel(
    other_ref, partial_ref, outside_ref, gain_ref, second_ref,
    predicted_in_ref, slope_in_ref, active_in_ref, normed_in_ref, inv_in_ref, first_ref,
    copies_ref, slope_ref, active_ref, normed_ref, inv_ref,
    own_ref,
):
    cells, width = normed_ref.shape
    core = lax.axis_index("co")
    last = cells - HALO
    inner, held = slice(HALO, last), slice(0, last - HALO)
    mine = pl.ds(pl.multiple_of(core * last, HALO), HALO)
    done = pl.ds(pl.multiple_of((1 - core) * last, HALO), HALO)
    summed = (partial_ref[...] + dot(outside_ref[...], other_ref[...])) * (1.0 / NEIGH)
    normed, inv_ref[mine, :] = normalise(summed, gain_ref[...])
    normed_ref[mine, :] = normed
    own_ref[...] = normed
    for full_ref, part_ref in (
        (normed_ref, normed_in_ref),
        (inv_ref, inv_in_ref),
        (active_ref, active_in_ref),
        (slope_ref, slope_in_ref),
    ):
        full_ref[inner, :] = part_ref[held, :]
        full_ref[done, :] = part_ref[last - HALO :, :]
    cols = 256
    for n in range(0, width, cols):
        part = slice(n, n + cols)
        active_ref[mine, part], slope_ref[mine, part] = head(own_ref, first_ref, part)
    predicted = dot(second_ref[...], active_ref[mine, :], 1, 1).astype(BF16)
    for m in range(copies_ref.shape[0]):
        copies_ref[m, :, inner] = predicted_in_ref[:, held]
        copies_ref[m, :, done] = predicted_in_ref[:, last - HALO :]
        copies_ref[m, :, mine] = predicted


def split_loss(tile, loss, fields):
    lane = lax.broadcasted_iota(jnp.int32, tile.shape, 1)
    high = loss.astype(BF16).astype(F32)
    low = loss - high
    return jnp.where(lane == fields, high, jnp.where(lane == fields + 1, low, tile))


def read_loss(tile, fields):
    lane = lax.broadcasted_iota(jnp.int32, tile.shape, 1)
    here = (lane == fields) | (lane == fields + 1)
    return jnp.sum(jnp.where(here, tile, 0.0), axis=1, keepdims=True)


def score_kernel(
    everyone_ref, target_ref, patch_ref, second_ref, slope_ref, active_ref, normed_ref,
    keep_ref, send_ref, dpre_ref,
):
    members, fields, cells = everyone_ref.shape
    width = slope_ref.shape[1]
    me = member_place(lax.axis_index("xh") * lax.axis_size("y") + lax.axis_index("y"), members)
    entries = fields * PATCH
    share = keep_ref.shape[2]

    def target_of(xl, member):
        return (member % 4) * 4 + (member // 4) * 2 + xl

    places = [(b, ((b // 2) % 2, b // 4)) for b in range(width // share)]
    own = everyone_ref[me].astype(F32)
    error = own - target_ref[...]
    sums = [jnp.sum(error * error, axis=0, keepdims=True)]
    for n in range(members):
        differ = own - everyone_ref[n].astype(F32)
        sums.append(jnp.sum(differ * differ, axis=0, keepdims=True))
    sums.append(jnp.zeros((16 - len(sums), cells), F32))
    sums = jnp.concatenate(sums, 0)
    even = (patch_ref[...] & 1) == 0
    spread_even = jnp.sqrt(jnp.sum(jnp.where(even, sums, 0.0), 1, keepdims=True) / entries + EPS_DIST)
    spread_odd = jnp.sqrt(jnp.sum(jnp.where(even, 0.0, sums), 1, keepdims=True) / entries + EPS_DIST)
    row = lax.broadcasted_iota(jnp.int32, (16, 1), 0)
    weight = jnp.where(row == 0, 1.0 / members, 1.0 / (members * (members - 1)))
    scale = jnp.where(even, weight / spread_even, weight / spread_odd)
    gradient = error * scale[0:1]
    for n in range(members):
        differ = own - everyone_ref[n].astype(F32)
        gradient = gradient - differ * scale[n + 1 : n + 2]
    both = spread_even + spread_odd
    used = jnp.where(row == 0, 1.0 / members, -0.5 / (members * (members - 1)))
    used = jnp.where((row == me + 1) | (row > members), 0.0, used)
    loss = jnp.sum(both * used, axis=0, keepdims=True)

    gradient = jnp.concatenate([gradient, jnp.zeros((LANES - fields, cells), F32)], 0)
    outer = gradient.T.astype(BF16)
    cols = 256
    for n in range(0, width, cols):
        part = slice(n, n + cols)
        d_active = dot(outer[:, :fields], second_ref[:, part])
        dpre_ref[:, part] = (d_active * slope_ref[:, part].astype(F32)).astype(BF16)

    def weight_grads(kept):
        for n in range(0, width, cols):
            grad = dot(normed_ref[...], dpre_ref[:, n : n + cols], 0, 0).astype(BF16)
            for band, slot in places:
                to_ref = keep_ref if band % 2 == kept else send_ref
                rows = grad[band * share : (band + 1) * share]
                for c in range(0, cols, LANES):
                    to_ref[target_of(slot[0], (n + c) // LANES), slot[1]] = rows[:, c : c + LANES]
        grad = dot(active_ref[...], outer, 0, 0)
        grad = split_loss(grad, loss, fields).astype(BF16)
        for band, slot in places:
            to_ref = keep_ref if band % 2 == kept else send_ref
            to_ref[target_of(slot[0], slot[1]), members] = grad[band * share : (band + 1) * share]

    core = lax.axis_index("co")
    pl.when(core == 0)(lambda: weight_grads(0))
    pl.when(core == 1)(lambda: weight_grads(1))


def backward_kernel(
    first_ref, dpre_ref, normed_ref, inv_ref, turned_ref, gain_ref,
    low_hbm, same_hbm, other_hbm,
    total_ref, low_ref, rim_ref, done,
):
    cells, width = low_ref.shape
    blocks = cells // HALO
    gain = gain_ref[...]
    inverse = 1.0 / gain
    core = lax.axis_index("co")
    saves = [
        pltpu.make_async_copy(source, place, done.at[i])
        for i, (source, place) in enumerate(
            [
                (rim_ref.at[0], same_hbm),
                (rim_ref.at[1], other_hbm),
                *(
                    (low_ref.at[i : i + HALO], low_hbm.at[i : i + HALO])
                    for i in range(0, cells, HALO)
                ),
            ]
        )
    ]
    cols = 256
    mean = jnp.zeros((cells, LANES), F32)
    along = jnp.zeros((cells, LANES), F32)
    for n in range(0, width, cols):
        part = slice(n, n + cols)
        d_normed = dot(dpre_ref[...], first_ref[:, part])
        scaled = d_normed * gain[:, part]
        total_ref[:, part] = scaled
        shared = d_normed * normed_ref[:, part].astype(F32)
        for c in range(0, cols, LANES):
            mean = mean + scaled[:, c : c + LANES]
            along = along + shared[:, c : c + LANES]
    mean = jnp.sum(mean, -1, keepdims=True)
    along = jnp.sum(along, -1, keepdims=True)
    for block in (0, blocks - 1, *range(1, blocks - 1)):
        own = slice(block * HALO, (block + 1) * HALO)
        inner = mean[own] * (1.0 / width) + normed_ref[own, :].astype(F32) * inverse * (
            along[own] * (1.0 / width)
        )
        low_ref[own, :] = (inv_ref[own, :1] * (total_ref[own, :] - inner)).astype(BF16)
        saves[2 + block].start()
        if block == 0:
            up = dot(turned_ref[:HALO, :HALO], low_ref[own, :]) * (1.0 / NEIGH)
            rim_ref[1 - core] = up.astype(BF16)
        if block == blocks - 1:
            down = dot(turned_ref[cells + HALO :, own], low_ref[own, :]) * (1.0 / NEIGH)
            rim_ref[core] = down.astype(BF16)
            saves[0].start()
            saves[1].start()
    for save in saves:
        save.wait()


def pair_kernel(fields, keep_ref, got_ref, out_ref):
    last = keep_ref.shape[1] - 1
    for k in range(keep_ref.shape[0]):
        total = keep_ref[k, :last].astype(F32) + got_ref[k, :last].astype(F32)
        out_ref[k, :last] = total.astype(BF16)
        tile = keep_ref[k, last].astype(F32) + got_ref[k, last].astype(F32)
        out_ref[k, last] = split_loss(tile, read_loss(tile, fields), fields).astype(BF16)


def plane_kernel(fields, parts_ref, out_ref):
    me = lax.axis_index("xh") * lax.axis_size("y") + lax.axis_index("y")
    blocks = parts_ref.shape[1] - 1
    for j in range(blocks + 1):
        total = parts_ref[0, j].astype(F32)
        for k in range(1, parts_ref.shape[0]):
            total = total + parts_ref[k, j].astype(F32)
        if j < blocks:
            out_ref[member_place(j, blocks), 0] = total.astype(BF16)
    loss = read_loss(total, fields)
    for j in range(blocks):
        tile = jnp.where(me == j, total, 0.0)
        out_ref[member_place(j, blocks), 1] = split_loss(tile, loss, fields).astype(BF16)


def fold_kernel(fields, parts_ref, out_ref):
    total = parts_ref[0].astype(F32)
    for k in range(1, parts_ref.shape[0]):
        total = total + parts_ref[k].astype(F32)
    first = total[0].astype(BF16)
    second = split_loss(total[1], read_loss(total[1], fields), fields).astype(BF16)
    for m in range(out_ref.shape[0]):
        out_ref[m, 0] = first
        out_ref[m, 1] = second


def last_kernel(fields, patches, parts_ref, first_ref, second_ref, loss_ref):
    members = parts_ref.shape[0]
    for m in range(members):
        first_ref[:, m * LANES : (m + 1) * LANES] = parts_ref[member_place(m, members), 0].astype(F32)
    tile = parts_ref[member_place(lax.axis_index("z"), members), 1].astype(F32)
    second_ref[...] = tile[:, :fields]
    loss_ref[...] = read_loss(tile, fields)[:1, :] * (1.0 / patches)


def gather_kernel(low_hbm, turned_hbm, same_ref, other_ref, grad_ref, low_ref, turned_ref, done):
    loads = [
        pltpu.make_async_copy(low_hbm, low_ref, done.at[0]),
        pltpu.make_async_copy(turned_hbm, turned_ref, done.at[1]),
    ]
    for load in loads:
        load.start()
    for load in loads:
        load.wait()
    core = lax.axis_index("co")
    blocks = low_ref.shape[0] // HALO
    for row in range(1, blocks + 1):
        near = slice(max(row - 2, 0) * HALO, min(row + 1, blocks) * HALO)
        back = dot(turned_ref[row * HALO : (row + 1) * HALO, near], low_ref[near, :]) * (1.0 / NEIGH)
        if row == 1:
            back = back + jnp.where(core == 0, other_ref[...], same_ref[...]).astype(F32)
        if row == blocks:
            back = back + jnp.where(core == 0, same_ref[...], other_ref[...]).astype(F32)
        grad_ref[(row - 1) * HALO : row * HALO, :] = back.astype(BF16)


BAND = ("z", "xl", "co")
MEM = ("xh", "y")
PLANE = ("y", "xh", "xl")


def member_groups(bands, members):
    groups = []
    for band in range(bands):
        group = [band * members + m for m in range(members)]
        groups.append(group if band % 2 == 0 else group[::-1])
    return groups


def height_groups(bands, members):
    groups = []
    for i in range(4 * members):
        group = [(z * 4 + i // members) * members + i % members for z in range(bands // 4)]
        groups.append(group if i // members % 2 == 0 else group[::-1])
    return groups


def member_place(member, members):
    return jnp.where(lax.axis_index("co") == 0, member, members - 1 - member)


def per_device(hidden, gain, w_first, w_second, target, patch_ids, neighbours):
    states = hidden[0]
    cells, width = states.shape
    fields = w_second.shape[1]
    bands, members = lax.axis_size(BAND), lax.axis_size(MEM)
    share = width // bands
    chips = [(i, i + 1) for i in range(1, bands - 1, 2)]
    chips = chips + [(j, i) for i, j in chips]
    cores = [(0, 1), (1, 0)]
    rim_same, rim_other = call(
        rims_kernel,
        [shape((HALO, width), BF16), shape((HALO, width), BF16)],
        [states],
        0,
        4,
        [pltpu.SemaphoreType.DMA((2,))],
        anywhere=(0,),
        held=(0, 1),
    )
    same = lax.ppermute(rim_same, "co", cores)
    other = lax.ppermute(rim_other, BAND, chips)
    held = cells - HALO
    saved = [shape((held, width), BF16)] * 3 + [shape((held, LANES), F32)]
    *inside, gain, first, second, partial, outside, turned, first_turned, turned_saved = call(
        inner_kernel,
        [
            shape((fields, held), BF16),
            *saved,
            shape((1, width), F32),
            shape(w_first.shape, BF16),
            shape((fields, width), BF16),
            shape((HALO, width), F32),
            shape((HALO, HALO), BF16),
            shape((cells + 2 * HALO, cells), BF16),
            shape(w_first.shape[::-1], BF16),
            shape((cells + 2 * HALO, cells), BF16),
        ],
        [same, neighbours, states, gain[None], w_first, w_second.T],
        10**9,
        16,
        [
            pltpu.VMEM(neighbours.shape, jnp.int32),
            pltpu.VMEM(states.shape, BF16),
            pltpu.SemaphoreType.DMA((6,)),
        ],
        anywhere=(1, 2, 3, 4, 5),
        stored=(12,),
        held=(5, 6, 7, 10, 11),
    )
    saved = [shape((cells, width), BF16)] * 3 + [shape((cells, LANES), F32)]
    copies, slope, active, normed, inv_root = call(
        outer_kernel,
        [shape((members, fields, cells), BF16)] + saved,
        [other, partial, outside, gain, second, *inside, first],
        10**9,
        20,
        [pltpu.VMEM((HALO, width), BF16)],
    )
    groups = member_groups(bands, members)
    everyone = lax.all_to_all(copies, BAND + MEM, 0, 0, axis_index_groups=groups)
    message = (2 * members, members + 1, share, LANES)
    keep, send, d_pre = call(
        score_kernel,
        [shape(message, BF16), shape(message, BF16), shape((cells, width), BF16)],
        [everyone, target, patch_ids[None], second, slope, active, normed],
        2 * 10**9,
        20,
    )
    got = lax.ppermute(send, "co", cores)
    low, rim_same, rim_other = call(
        backward_kernel,
        [
            shape((cells, width), BF16),
            shape((HALO, width), BF16),
            shape((HALO, width), BF16),
        ],
        [first_turned, d_pre, normed, inv_root, turned, gain],
        2 * 10**9,
        20,
        [
            pltpu.VMEM((cells, width), F32),
            pltpu.VMEM((cells, width), BF16),
            pltpu.VMEM((2, HALO, width), BF16),
            pltpu.SemaphoreType.DMA((2 + cells // HALO,)),
        ],
        stored=(0, 1, 2),
    )
    got, low = lax.optimization_barrier((got, low))
    (mine,) = call(
        functools.partial(pair_kernel, fields), [shape(message, BF16)], [keep, got], 10**6, 8
    )
    parts = lax.all_to_all(mine, PLANE, 0, 0)
    parts, rim_same, rim_other = lax.optimization_barrier((parts, rim_same, rim_other))
    same = lax.ppermute(rim_same, "co", cores)
    other = lax.ppermute(rim_other, BAND, chips)
    (grad_hidden,) = call(
        gather_kernel,
        [shape((cells, width), BF16)],
        [low, turned_saved, same, other],
        0,
        16,
        [
            pltpu.VMEM((cells, width), BF16),
            pltpu.VMEM(turned.shape, BF16),
            pltpu.SemaphoreType.DMA((2,)),
        ],
        anywhere=(0, 1),
    )
    message = (members, 2, share, LANES)
    (planed,) = call(
        functools.partial(plane_kernel, fields), [shape(message, BF16)], [parts], 10**6, 8
    )
    heights = height_groups(bands, members)
    parts = lax.all_to_all(planed, BAND + MEM, 0, 0, axis_index_groups=heights)
    (folded,) = call(
        functools.partial(fold_kernel, fields), [shape(message, BF16)], [parts], 10**6, 8
    )
    parts = lax.all_to_all(folded, BAND + MEM, 0, 0, axis_index_groups=groups)
    grad_first, grad_second, loss = call(
        functools.partial(last_kernel, fields, cells // PATCH * bands),
        [shape((share, width), F32), shape((share, fields), F32), shape((1, 1), F32)],
        [parts],
        10**6,
        8,
    )
    return (loss[0, 0], grad_hidden[None], grad_first, grad_second)


def solution(mesh):
    split = jax.sharding.Mesh(mesh.devices.reshape(8, 2, 2, 2, 4), BAND + MEM)
    return jax.shard_map(
        per_device,
        mesh=split,
        in_specs=(
            P(MEM, BAND, None),
            P(),
            P(),
            P(),
            P(None, BAND),
            P(BAND),
            P(None, BAND),
        ),
        out_specs=(P(), P(MEM, BAND, None), P(BAND, None), P(BAND, None)),
        check_vma=False,
    )
```
